32 devices in a mesh: req: 4 (over z), exp: 8 (over y, x, core).
Axes of the slice: x: 2, y: 2, z: 4, core: 2. Of those that a mesh axis runs over, the one named last changes fastest.
Arguments:
- queries: bfloat16 [512, 9216], P('req', 'exp'), may hold values from -8 to 8
- new_latent: bfloat16 [512, 576], P('req'), may hold values from -6 to 6
- pool: bfloat16 [128, 36864], P('req'), may hold values from -5 to 5
- page_list: int32 [8, 16], replicated, may hold values from 0 to 127, as said below
- prefix_len: int32 [8], replicated, may hold values from 1 to 1024, as said below
- hidden_in: bfloat16 [512, 7168], P(('req', 'exp')), may hold values from -6 to 6
- norm_gain: bfloat16 [7168], replicated, may hold values from 0.5 to 1.5
- uv_weight: bfloat16 [16, 512, 128], P('exp'), may hold values from -0.25 to 0.25
- out_weight: bfloat16 [2048, 7168], P('exp', 'req'), may hold values from -1 to 1
- route_ids: int32 [512, 8], P('req'), may hold values from 0 to 7, all different within a row; in each aligned block of 128 rows (0 to 127, 128 to 255, ...) at most 128 rows name the same one
- route_weight: float32 [512, 8], P('req'), may hold values from 0.05 to 0.6
- gate_weight: bfloat16 [8, 7168, 2048], P('exp', None, 'req'), may hold values from -0.0625 to 0.0625
- up_weight: bfloat16 [8, 7168, 2048], P('exp', None, 'req'), may hold values from -0.0625 to 0.0625
- down_weight: bfloat16 [8, 2048, 7168], P('exp', 'req'), may hold values from -0.125 to 0.125
Outputs:
- mixed: bfloat16 [512, 7168], P(('req', 'exp'))
The draws below stay inside these ranges and needn't reach their ends.
Inputs may be any that keep to these rules, and one draw needn't show every extreme that they name: `page_list`: pool row p is held by req index p // 32. The page at position j of a list lies at depth j of a radix tree with ids j * 8 to j * 8 + 7 at that depth; two lists that share the page at position j share all earlier positions. Counting only positions j < ceil(prefix_len / 64), the 2 requests of one req index (rows r * 2 onward) need at most 8 distinct pages held by one req index, and some req index needs exactly 8 from some holder. `prefix_len`: every request has at least one cached token; some req index has all its requests at the full 16 * 64 cached tokens. `route_ids`: in each block of 128 rows (the tokens of one req index) no expert is named by more than 128 rows, a bound that some block reaches.
All inputs are finite; a program needn't handle non-finite values.
Results may differ from the reference program's by a relative error of at most 0.023.
Values may be sent and summed in bfloat16 or wider, within the bound.
No kernel may reach another device: no remote copies, remote signals or barrier semaphores. Data moves between devices by JAX's collectives and lax.ppermute only.
A program may use at most 64 MiB of HBM per device.

```python
import math
import jax
import jax.numpy as jnp
import numpy as np
from jax import lax

D = 7168
KVR = 512
LAT = 576
VDIM = 128
FFE = 2048
TOPK = 8
HEAD_DEV = 2
HEADS = 16
EXPERTS = 8
PAGE = 64
BRANCH = 8
PMAX = 16
REQ_R = 2
NEW = 64
TOK_R = 128
TOKENS = 512
REQUESTS = 8
POOL = 128
CAP = 128
N_REQ = 4
N_EXP = 8


def tree_star(key):
    return jax.random.randint(jax.random.fold_in(key, 5), (), 0, N_REQ)


def draw_page_list(key, part):
    star = tree_star(key)
    codes = jax.random.randint(jax.random.fold_in(key, 6), (REQUESTS,), 0, BRANCH)
    request_ids = jnp.arange(REQUESTS, dtype=jnp.int32)
    codes = jnp.where(request_ids // REQ_R == star, jnp.bitwise_xor(BRANCH - 1, request_ids % REQ_R), codes)
    logw = BRANCH.bit_length() - 1
    depth_ids = jnp.arange(PMAX, dtype=jnp.int32)
    bits_used = jnp.minimum(logw, depth_ids * (logw + 1) // PMAX)
    branch_ids = jnp.right_shift(codes[:, None], logw - bits_used[None, :])
    return (depth_ids[None, :] * BRANCH + branch_ids).astype(jnp.int32)


def draw_prefix_len(key, part):
    star = tree_star(key)
    lengths = jax.random.randint(jax.random.fold_in(key, 8), (REQUESTS,), 1, PMAX * PAGE + 1)
    request_ids = jnp.arange(REQUESTS, dtype=jnp.int32)
    return jnp.where(request_ids // REQ_R == star, PMAX * PAGE, lengths).astype(jnp.int32)


def draw_pool(key, part):
    pool_shape = (POOL, PAGE * LAT)
    values = jnp.clip(jax.random.normal(jax.random.fold_in(key, 21), pool_shape, jnp.float32), -5.0, 5.0)
    return values.astype(jnp.bfloat16)


def draw_queries(key, part):
    query_shape = (TOKENS, HEADS, LAT)
    values = jnp.clip(jax.random.normal(jax.random.fold_in(key, 31), query_shape, jnp.float32), -8.0, 8.0)
    return values.reshape(TOKENS, HEADS * LAT).astype(jnp.bfloat16)


def block_scale(stream_key, extent, shards, low, largest):
    gain = 1.0
    for position, parts in shards:
        heights = jax.random.uniform(jax.random.fold_in(jax.random.fold_in(stream_key, 6), position), (parts,), jnp.float32, low / len(shards), largest / len(shards))
        gain = gain * jnp.repeat(jnp.exp(heights), extent[position] // parts).reshape((-1,) + (1,) * (len(extent) - 1 - position))
    return gain


def shared_out(key, own, number, rows, amount, top, limit, lean):
    order = jax.random.permutation(key, amount)
    crowded, usual = load_shares(amount, rows * top, limit, lean, True), load_shares(amount, rows * top, limit, lean, False)
    places = jnp.arange(amount)

    def named(sizes, rotation):
        used = int((sizes > 0).sum())
        fixed = max(1, used // 4)
        passed = fixed + (places - fixed + rotation * (used - fixed)) % max(1, amount - fixed)
        return jnp.zeros((amount,), jnp.int32).at[order[jnp.where(places < fixed, places, passed)]].set(jnp.asarray(sizes, jnp.int32))

    sizes = jnp.where(number % 4 == 0, named(crowded, number // 4), named(usual, number - number // 4 - 1))
    mixed = jax.random.permutation(jax.random.fold_in(own, 3), amount)
    source_of, taker = mixed[0:amount // 2 * 2:2], mixed[1:amount // 2 * 2:2]
    room = jnp.minimum(sizes[source_of] - 1, limit - sizes[taker]) // 2
    room = jnp.where((source_of == order[0]) | (taker == order[0]) | (sizes[taker] == 0), 0, jnp.maximum(room, 0))
    passed = jax.random.randint(jax.random.fold_in(own, 4), (amount // 2,), 0, 1 << 20) % (room + 1)
    sizes = sizes.at[source_of].add(-passed).at[taker].add(passed)
    members = jnp.searchsorted(jnp.cumsum(sizes), jnp.arange(rows * top), side="right").astype(jnp.int32)
    listing = members.reshape(top, rows).T
    listing = listing[jax.random.permutation(jax.random.fold_in(own, 1), rows)]
    rotation = jax.random.randint(jax.random.fold_in(own, 2), (rows, 1), 0, top)
    return jnp.take_along_axis(listing, (jnp.arange(top)[None, :] + rotation) % top, axis=1)


def load_shares(amount, total, bound, lean, full):
    loads = [(1 << 20) // math.isqrt(grade ** lean) + 1 for grade in range(1, amount + 1)]
    largest = bound if full else min(bound, max(-(-total // amount), total * loads[0] // sum(loads)))
    least = 1 if total - largest >= amount - 1 else 0
    counts, spare = [largest] + [least] * (amount - 1), total - largest - least * (amount - 1)
    while spare > 0:
        candidates = [i for i in range(1, amount) if counts[i] < largest] or [i for i in range(1, amount) if counts[i] < bound]
        mass, budget = sum([loads[i] for i in candidates]), spare
        for i in candidates:
            extra = min(bound - counts[i], max(1, budget * loads[i] // mass), spare)
            counts[i] = counts[i] + extra
            spare = spare - extra
    return np.array(counts)


def scatter_about(key, dims, width, reach, pieces=(), kind=jnp.bfloat16):
    array = jax.random.normal(key, dims, jnp.float32) * width
    if len(pieces) > 0:
        array = block_scale(key, dims, pieces, -0.22, 0.18) * array
    return jnp.clip(array, min=-reach, max=reach).astype(kind)


def setup_inputs(seed: int = 0) -> dict:
    seeds = jax.random.split(jax.random.key(seed), 15)
    queries = draw_queries(jax.random.fold_in(seeds[14], 71), 0)
    new_latent = scatter_about(seeds[1], (TOKENS, LAT), 1.0, 6.0, ((0, 4),))
    pool = draw_pool(jax.random.fold_in(seeds[14], 71), 0)
    page_list = draw_page_list(jax.random.fold_in(seeds[14], 71), 0)
    prefix_len = draw_prefix_len(jax.random.fold_in(seeds[14], 71), 0)
    hidden_in = scatter_about(seeds[5], (TOKENS, D), 1.0, 6.0, ((0, 32),))
    norm_gain = jnp.clip(1.0 + 0.1 * jax.random.normal(seeds[6], (D,), jnp.float32), 0.5, 1.5).astype(jnp.bfloat16)
    uv_weight = scatter_about(seeds[7], (HEADS, KVR, VDIM), KVR ** -0.5, 0.25, ((0, 8),))
    out_weight = scatter_about(seeds[8], (HEADS * VDIM, D), (HEADS * VDIM // 64) ** -0.5, 1.0, ((0, 8), (1, 4)))
    route_ids_keys = jax.random.split(jax.random.fold_in(seeds[9], 1), TOKENS // TOK_R)
    route_ids_turns = jax.random.permutation(jax.random.fold_in(seeds[9], 3), TOKENS // TOK_R)
    route_ids = jax.vmap(lambda own, number: shared_out(jax.random.fold_in(seeds[9], 2), own, number, TOK_R, EXPERTS, TOPK, CAP, 2))(route_ids_keys, route_ids_turns).reshape((TOKENS, TOPK))
    route_weight = jnp.clip(jnp.exp(math.log(0.6) - 2.4849067 * jax.random.uniform(seeds[10], (TOKENS, TOPK), jnp.float32) ** block_scale(seeds[10], (TOKENS, TOPK), ((0, 4),), -0.2, 0.2)), 0.05, 0.6)
    gate_weight = scatter_about(seeds[11], (EXPERTS, D, FFE), D ** -0.5, 0.0625, ((0, 8), (2, 4)))
    up_weight = scatter_about(seeds[12], (EXPERTS, D, FFE), D ** -0.5, 0.0625, ((0, 8), (2, 4)))
    down_weight = scatter_about(seeds[13], (EXPERTS, FFE, D), FFE ** -0.5, 0.125, ((0, 8), (1, 4)))
    return {"queries": queries, "new_latent": new_latent, "pool": pool, "page_list": page_list, "prefix_len": prefix_len, "hidden_in": hidden_in, "norm_gain": norm_gain, "uv_weight": uv_weight, "out_weight": out_weight, "route_ids": route_ids, "route_weight": route_weight, "gate_weight": gate_weight, "up_weight": up_weight, "down_weight": down_weight}


score_scale = 192.0 ** (-0.5)
norm_eps = 1e-06

def attend_request(query_block, key_block, length):
    scores = jnp.einsum('thc,kc->thk', query_block.astype(jnp.float32), key_block.astype(jnp.float32)) * score_scale
    key_pos = jnp.arange(key_block.shape[0], dtype=jnp.int32)
    tok_pos = jnp.arange(NEW, dtype=jnp.int32)
    prefix_total = PMAX * PAGE
    visible = jnp.where(key_pos[None, :] < prefix_total, key_pos[None, :] < length, key_pos[None, :] - prefix_total <= tok_pos[:, None])
    scores = jnp.where(visible[:, None, :], scores, -1e+30)
    row_max = lax.optimization_barrier(jnp.max(scores, axis=-1, keepdims=True))
    exp_scores = jnp.exp(scores - row_max)
    soft_probs = (exp_scores / lax.optimization_barrier(jnp.sum(exp_scores, axis=-1, keepdims=True))).astype(jnp.bfloat16)
    values = key_block[:, :KVR].astype(jnp.float32)
    return jnp.einsum('thk,kc->thc', soft_probs.astype(jnp.float32), values).astype(jnp.bfloat16)

def reference(queries, new_latent, pool, page_list, prefix_len, hidden_in, norm_gain, uv_weight, out_weight, route_ids, route_weight, gate_weight, up_weight, down_weight):
    query_blocks = queries.reshape(REQUESTS, NEW, HEADS, LAT)
    page_keys = pool[page_list].reshape(REQUESTS, PMAX * PAGE, LAT)
    all_keys = jnp.concatenate([page_keys, new_latent.reshape(REQUESTS, NEW, LAT)], axis=1)
    latent_out = lax.map(lambda packed: attend_request(packed[0], packed[1], packed[2]), (query_blocks, all_keys, prefix_len))
    head_out = jnp.einsum('rthc,hcv->rthv', latent_out.astype(jnp.float32), uv_weight.astype(jnp.float32)).astype(jnp.bfloat16)
    head_out = head_out.reshape(TOKENS, HEADS * VDIM)
    group_width = HEAD_DEV * VDIM

    def add_group(total, group_idx):
        columns = lax.dynamic_slice_in_dim(head_out, (group_idx * group_width).astype(jnp.int32), group_width, 1)
        weight_rows = lax.dynamic_slice_in_dim(out_weight, (group_idx * group_width).astype(jnp.int32), group_width, 0)
        term = jnp.dot(columns, weight_rows, preferred_element_type=jnp.float32)
        term = lax.optimization_barrier(term.astype(jnp.bfloat16)).astype(jnp.float32)
        return (total + term, None)
    attn, unused = lax.scan(add_group, jnp.zeros((TOKENS, D), jnp.float32), jnp.arange(N_EXP, dtype=jnp.int32))
    resid = (hidden_in.astype(jnp.float32) + attn).astype(jnp.bfloat16)
    widened = resid.astype(jnp.float32)
    inv_scale = lax.rsqrt(lax.optimization_barrier(jnp.mean(widened * widened, axis=-1, keepdims=True)) + norm_eps)
    normed = (widened * inv_scale * norm_gain.astype(jnp.float32)).astype(jnp.bfloat16)
    group_routes = route_ids.reshape(N_REQ, TOK_R, TOPK)
    group_weights = route_weight.reshape(N_REQ, TOK_R, TOPK)
    normed_groups = normed.reshape(N_REQ, TOK_R, D).astype(jnp.float32)
    slice_width = FFE // N_REQ
    slot_ids = jnp.arange(CAP, dtype=jnp.int32)

    def add_expert(total, inputs):
        gate_here, up_here, down_here, expert_id = inputs
        chosen = group_routes == expert_id
        routed = jnp.any(chosen, axis=2)
        token_weight = lax.optimization_barrier(jnp.sum(jnp.where(chosen, group_weights, 0.0), axis=2))
        slot_order = jnp.cumsum(routed.astype(jnp.int32), axis=1).astype(jnp.int32) - 1
        placing = (routed[:, None, :] & (slot_order[:, None, :] == slot_ids[None, :, None])).astype(jnp.float32)
        expert_in = jnp.einsum('gst,gtd->gsd', placing, normed_groups).astype(jnp.bfloat16).reshape(N_REQ * CAP, D)
        gate_val = jnp.dot(expert_in, gate_here, preferred_element_type=jnp.float32)
        up_val = jnp.dot(expert_in, up_here, preferred_element_type=jnp.float32)
        active = (jax.nn.silu(gate_val) * up_val).astype(jnp.bfloat16)
        expert_sum = jnp.zeros((N_REQ * CAP, D), jnp.float32)
        for slice_idx in range(N_REQ):
            piece_out = jnp.dot(active[:, slice_idx * slice_width:(slice_idx + 1) * slice_width], down_here[slice_idx * slice_width:(slice_idx + 1) * slice_width], preferred_element_type=jnp.float32)
            expert_sum = expert_sum + lax.optimization_barrier(piece_out.astype(jnp.bfloat16)).astype(jnp.float32)
        expert_out = expert_sum.astype(jnp.bfloat16).reshape(N_REQ, CAP, D)
        slot_weight = jnp.einsum('gst,gt->gs', placing, token_weight, precision=lax.Precision.HIGHEST)
        weighted = lax.optimization_barrier((slot_weight[:, :, None] * expert_out.astype(jnp.float32)).astype(jnp.bfloat16))
        expert_terms = jnp.einsum('gst,gsd->gtd', placing, weighted.astype(jnp.float32)).reshape(TOKENS, D)
        return (total + expert_terms, None)
    moe, unused = lax.scan(add_expert, jnp.zeros((TOKENS, D), jnp.float32), (gate_weight, up_weight, down_weight, jnp.arange(EXPERTS, dtype=jnp.int32)))
    return (resid.astype(jnp.float32) + moe).astype(jnp.bfloat16)
```

```python
import jax
import jax.numpy as jnp
from jax import lax
from jax.sharding import PartitionSpec as P

score_scale = 192.0 ** (-0.5)
norm_eps = 1e-06
chunk_count = 2


def swap(x, axis, distance):
    size = lax.axis_size(axis)
    return lax.ppermute(x, axis, [(i, i ^ distance) for i in range(size)])


def local(
    queries,
    new_latent,
    pool,
    page_list,
    prefix_len,
    hidden_in,
    norm_gain,
    uv_weight,
    out_weight,
    route_ids,
    route_weight,
    gate_weight,
    up_weight,
    down_weight,
):
    req_count = lax.axis_size("req")
    exp_count = lax.axis_size("exp")
    req_index = lax.axis_index("req")
    exp_index = lax.axis_index("exp")
    tok_rows = queries.shape[0]
    latent = new_latent.shape[1]
    kv_rank = uv_weight.shape[1]
    value_width = uv_weight.shape[2]
    head_here = uv_weight.shape[0]
    pool_rows = pool.shape[0]
    page_size = pool.shape[1] // latent
    list_depth = page_list.shape[1]
    per_index = page_list.shape[0] // req_count
    depth_here = list_depth // req_count
    width = hidden_in.shape[1]
    col_width = width // req_count
    half_width = width // 2
    own_rows = tok_rows // exp_count
    sub_rows = own_rows // chunk_count
    outer = exp_count // 2
    req_rel = req_index ^ jnp.arange(req_count, dtype=jnp.int32)
    rel_order = [2 * k for k in range(outer)] + [2 * k + 1 for k in range(outer)]
    exp_rel = exp_index ^ jnp.array(rel_order, dtype=jnp.int32)

    slot_count = per_index * depth_here
    parts = max(1, exp_count // slot_count)
    unit_tokens = page_size // parts
    unit_width = unit_tokens * latent
    per_group = exp_count // per_index
    pieces = pool.reshape(pool_rows * parts, unit_width)
    page_lists = page_list.reshape(req_count, per_index, list_depth)
    lengths = prefix_len.reshape(req_count, per_index)

    def unit_row(target, unit):
        request = unit // per_group
        depth = req_index * depth_here + (unit // parts) % depth_here
        page = page_lists[target, request, depth] - req_index * pool_rows
        return jnp.clip(page, 0, pool_rows - 1) * parts + unit % parts

    send_rows = unit_row(req_rel[1:], exp_index)
    units = exp_index ^ jnp.arange(exp_count, dtype=jnp.int32)
    own_units = unit_row(req_index, units)
    wanted = jnp.concatenate([send_rows, own_units])
    picker = (wanted[:, None] == jnp.arange(pool_rows * parts, dtype=jnp.int32)).astype(
        jnp.bfloat16
    )
    picked = jnp.dot(picker, pieces, preferred_element_type=jnp.float32).astype(jnp.bfloat16)
    far = [swap(picked[j - 1 : j], "req", j) for j in range(1, req_count)]
    far = jnp.concatenate(far, axis=0)
    far_out = jnp.stack([far] + [swap(far, "exp", 2 * k) for k in range(1, outer)])
    far_other = swap(far_out, "exp", 1)
    far_all = jnp.stack([far_out, far_other], axis=1).reshape(
        exp_count, req_count - 1, unit_width
    )
    near = picked[req_count - 1 :].reshape(exp_count, 1, unit_width)
    fetched = jnp.concatenate([near, far_all], axis=1)
    group_keys = fetched.reshape(per_index, per_group * req_count * unit_tokens, latent)
    first = exp_index // per_group
    group_request = first ^ jnp.arange(per_index, dtype=jnp.int32)
    unit_ids = units.reshape(per_index, per_group, 1, 1)
    group_pos = (
        (req_rel[None, None, :, None] * depth_here + (unit_ids // parts) % depth_here) * page_size
        + (unit_ids % parts) * unit_tokens
        + jnp.arange(unit_tokens, dtype=jnp.int32)
    ).reshape(per_index, -1)
    my_lengths = lax.dynamic_index_in_dim(lengths, req_index, 0, keepdims=False)[group_request]
    new_count = tok_rows // per_index
    new_keys = new_latent.reshape(per_index, new_count, latent)[group_request]
    all_keys = jnp.concatenate([group_keys, new_keys], axis=1)
    query_blocks = queries.reshape(per_index, new_count, head_here, latent)[group_request]
    scores = (
        jnp.einsum("rthc,rkc->rthk", query_blocks, all_keys, preferred_element_type=jnp.float32)
        * score_scale
    )
    tok_pos = jnp.arange(new_count, dtype=jnp.int32)
    seen_old = jnp.broadcast_to(
        (group_pos < my_lengths[:, None])[:, None, :],
        (per_index, new_count, group_pos.shape[1]),
    )
    seen_new = jnp.broadcast_to(
        (tok_pos[None, :] <= tok_pos[:, None])[None], (per_index, new_count, new_count)
    )
    visible = jnp.concatenate([seen_old, seen_new], axis=2)
    scores = jnp.where(visible[:, :, None, :], scores, -1e30)
    row_max = jnp.max(scores, axis=-1, keepdims=True)
    exp_scores = jnp.exp(scores - row_max)
    soft_probs = (exp_scores / jnp.sum(exp_scores, axis=-1, keepdims=True)).astype(jnp.bfloat16)
    latent_out = jnp.einsum(
        "rthk,rkc->rthc", soft_probs, all_keys[:, :, :kv_rank], preferred_element_type=jnp.float32
    ).astype(jnp.bfloat16)
    head_out = jnp.einsum(
        "rthc,hcv->rthv", latent_out, uv_weight, preferred_element_type=jnp.float32
    ).astype(jnp.bfloat16)
    head_out = head_out[group_request].reshape(
        exp_count, chunk_count, sub_rows, head_here * value_width
    )[exp_rel]
    head_out = head_out.transpose(1, 0, 2, 3)

    chosen = route_ids == exp_index
    token_weight = jnp.sum(jnp.where(chosen, route_weight, 0.0), axis=1)
    token_weight = token_weight.reshape(exp_count, chunk_count, sub_rows)[exp_rel]
    weight_all = jnp.stack(
        [token_weight] + [swap(token_weight, "req", j) for j in range(1, req_count)]
    ).transpose(2, 1, 0, 3)

    hidden_cols = []
    for j in range(req_count):
        piece = lax.dynamic_slice_in_dim(hidden_in, req_rel[j] * col_width, col_width, 1)
        hidden_cols.append(piece if j == 0 else swap(piece, "req", j))
    hidden_cols = jnp.stack(hidden_cols).reshape(req_count, chunk_count, sub_rows, col_width)

    heads_all = jnp.stack(
        [head_out] + [swap(head_out, "req", j) for j in range(1, req_count)], axis=2
    )
    block = req_count * sub_rows

    def front(c):
        partial = jnp.dot(
            heads_all[c].reshape(exp_count * block, -1),
            out_weight,
            preferred_element_type=jnp.float32,
        )
        cut = outer * block
        other = swap(partial[cut:].astype(jnp.bfloat16), "exp", 1)
        pair = (partial[:cut] + other.astype(jnp.float32)).astype(jnp.bfloat16)
        pair = pair.reshape(outer, block, col_width)
        total = pair[0].astype(jnp.float32)
        for k in range(1, outer):
            total = total + swap(pair[k], "exp", 2 * k).astype(jnp.float32)
        resid = hidden_cols[:, c].astype(jnp.float32) + total.reshape(
            req_count, sub_rows, col_width
        )
        resid = resid.astype(jnp.bfloat16)
        slices = [resid]
        for j in range(1, req_count):
            got = swap(resid, "req", j)
            slices.append(jnp.stack([got[i ^ j] for i in range(req_count)]))
        ordered = jnp.stack(slices)[req_rel]
        full = ordered.transpose(1, 2, 0, 3).reshape(block, width)
        widened = full.astype(jnp.float32)
        inv_scale = lax.rsqrt(jnp.mean(widened * widened, axis=-1, keepdims=True) + norm_eps)
        normed = (widened * inv_scale * norm_gain.astype(jnp.float32)).astype(jnp.bfloat16)
        return full[:sub_rows], normed

    outer_bits = []
    bit = 1
    while bit < outer:
        outer_bits.append(bit)
        bit *= 2

    def gather_plane(piece, bits):
        blocks = {0: piece}
        for bit in bits:
            for k in list(blocks):
                blocks[k ^ bit] = swap(blocks[k], "exp", 2 * bit)
        same = [blocks[k] for k in range(outer)]
        other = [swap(b, "exp", 1) for b in same]
        return jnp.concatenate(same + other, axis=0)

    def scatter_plane(partial, bits):
        cut = outer * block
        other = swap(partial[cut:].astype(jnp.bfloat16), "exp", 1)
        pair = (partial[:cut] + other.astype(jnp.float32)).reshape(outer, block, half_width)
        blocks = {k: pair[k] for k in range(outer)}
        for bit in bits:
            kept = {}
            for k in [k for k in blocks if not k & bit]:
                got = swap(blocks[k ^ bit].astype(jnp.bfloat16), "exp", 2 * bit)
                kept[k] = blocks[k] + got.astype(jnp.float32)
            blocks = kept
        return blocks[0].astype(jnp.bfloat16)

    gate_here = gate_weight[0]
    up_here = up_weight[0]
    down_here = down_weight[0]

    def experts(left, right, weights):
        def project(matrix):
            return jnp.dot(
                left, matrix[:half_width], preferred_element_type=jnp.float32
            ) + jnp.dot(right, matrix[half_width:], preferred_element_type=jnp.float32)

        active = (jax.nn.silu(project(gate_here)) * project(up_here)).astype(jnp.bfloat16)
        outs = []
        for matrix in (down_here[:, :half_width], down_here[:, half_width:]):
            out = jnp.dot(active, matrix, preferred_element_type=jnp.float32)
            outs.append(out * weights[:, None])
        return outs

    results = []
    for c in range(chunk_count):
        resid_own, normed = front(c)
        left = gather_plane(normed[:, :half_width], outer_bits)
        right = gather_plane(normed[:, half_width:], outer_bits[::-1])
        out_left, out_right = experts(left, right, weight_all[c].reshape(-1))
        total = resid_own.astype(jnp.float32)
        sides = []
        for partial, bits in ((out_left, outer_bits), (out_right, outer_bits[::-1])):
            sums = scatter_plane(partial, bits).reshape(req_count, sub_rows, half_width)
            side = sums[0].astype(jnp.float32)
            for j in range(1, req_count):
                side = side + swap(sums[j], "req", j).astype(jnp.float32)
            sides.append(side)
        total = total + jnp.concatenate(sides, axis=1)
        results.append(total.astype(jnp.bfloat16))
    return jnp.concatenate(results, axis=0)


def solution(mesh):
    return jax.shard_map(
        local,
        mesh=mesh,
        in_specs=(
            P("req", "exp"),
            P("req", None),
            P("req", None),
            P(),
            P(),
            P(("req", "exp"), None),
            P(),
            P("exp", None, None),
            P("exp", "req"),
            P("req", None),
            P("req", None),
            P("exp", None, "req"),
            P("exp", None, "req"),
            P("exp", "req", None),
        ),
        out_specs=P(("req", "exp"), None),
        check_vma=False,
    )
```

```python
import functools

import jax
import jax.numpy as jnp
import numpy as np
from jax import lax
from jax.experimental import pallas as pl
from jax.experimental.pallas import tpu as pltpu
from jax.sharding import PartitionSpec as P

score_scale = 192.0 ** (-0.5)
norm_eps = 1e-06
chunk_count = 2


def swap(x, axis, distance):
    size = lax.axis_size(axis)
    return lax.ppermute(x, axis, [(i, i ^ distance) for i in range(size)])


def pick_kernel(plan, place, lists, pool, *outs):
    req_count, per_index, depth_here, pool_rows, width, far_width, far_split, near_split = plan
    slots = per_index * depth_here
    req_index, exp_index = place[0], place[1]
    row = lax.broadcasted_iota(jnp.int32, (16, pool_rows), 0)
    column = lax.broadcasted_iota(jnp.int32, (16, pool_rows), 1)

    def wanted(target):
        hot = row < 0
        for slot in range(slots):
            request, depth = slot // depth_here, slot % depth_here
            page = lists[target * per_index + request, req_index * depth_here + depth]
            hot = hot | ((row == slot) & (column == page - req_index * pool_rows))
        return hot.astype(jnp.float32)

    def lay(hot, start, split, piece):
        total = jnp.zeros((16, piece), jnp.float32)
        for part in range(split):
            shifted = hot if part == 0 else pltpu.roll(hot, part * slots, 0)
            cols = pl.ds(pl.multiple_of(start + part * piece, 128), piece)
            total = total + jnp.dot(
                shifted.astype(jnp.bfloat16), pool[:, cols], preferred_element_type=jnp.float32
            )
        return total.astype(jnp.bfloat16)

    for out, j in zip(outs, range(1, req_count)):
        out[...] = lay(
            wanted(req_index ^ j), exp_index * far_width, far_split, far_width // far_split
        )


def near_kernel(plan, place, lists, pool, out):
    req_count, per_index, depth_here, pool_rows, width, far_width, far_split, near_split = plan
    slots = per_index * depth_here
    req_index = place[0]
    row = lax.broadcasted_iota(jnp.int32, (16, pool_rows), 0)
    column = lax.broadcasted_iota(jnp.int32, (16, pool_rows), 1)
    hots = [row < 0] * near_split
    for slot in range(slots):
        request, depth = slot // depth_here, slot % depth_here
        page = lists[req_index * per_index + request, req_index * depth_here + depth]
        here = column == page - req_index * pool_rows
        for part in range(near_split):
            hots[part] = hots[part] | ((row == part * slots + slot) & here)
    hots = [hot.astype(jnp.float32).astype(jnp.bfloat16) for hot in hots]
    piece = width // near_split
    step = 1152
    for start in range(0, piece, step):
        total = jnp.zeros((16, step), jnp.float32)
        for part in range(near_split):
            cols = slice(part * piece + start, part * piece + start + step)
            total = total + jnp.dot(hots[part], pool[:, cols], preferred_element_type=jnp.float32)
        out[:, start : start + step] = total.astype(jnp.bfloat16)


def attention_kernel(
    plan, place, near, far, new, q_even, q_odd, bias_even, bias_odd, bias_new, uv, out,
    k_even, k_odd, s_even, s_odd, heads,
):
    per_index, latent, kv_rank, head_here, tok_rows, order, sub_rows, chunks = plan
    pair = 2 * latent
    window = latent + 64
    lead = pair - window
    units, far_rows, far_width = far.shape
    near_rows = near.shape[0]
    base = 0

    def place_keys(rows, value_of, pairs, base):
        for p in range(pairs):
            k_even[base : base + rows, :] = value_of(p * pair, p * pair + window)
            k_odd[base : base + rows, :] = value_of(p * pair + lead, (p + 1) * pair)
            base += rows
        return base

    base = place_keys(near_rows, lambda a, b: near[:, a:b], near.shape[1] // pair, base)
    for m in range(units):
        base = place_keys(far_rows, lambda a, b: far[m, :, a:b], far_width // pair, base)
    rows_k = (((1,), (1,)), ((), ()))

    def times(a, b):
        return lax.dot_general(a, b, rows_k, preferred_element_type=jnp.float32) * score_scale

    s_even[...] = times(q_even[...], k_even[...])
    s_odd[...] = times(q_odd[...], k_odd[...])
    s_new = times(q_even[...], new[...])
    new_count = tok_rows // per_index
    p_even, p_odd, p_new = [], [], []
    for h in range(head_here):
        for i in range(per_index):
            at = h * tok_rows + i * new_count
            rows = slice(at, at + new_count)
            even = s_even[rows, :] + bias_even[i : i + 1, :]
            odd = s_odd[rows, :] + bias_odd[i : i + 1, :]
            fresh = s_new[rows, :] + bias_new[i * new_count : (i + 1) * new_count, :]
            top = jnp.maximum(
                jnp.max(jnp.maximum(even, odd), axis=-1, keepdims=True),
                jnp.max(fresh, axis=-1, keepdims=True),
            )
            even, odd, fresh = jnp.exp(even - top), jnp.exp(odd - top), jnp.exp(fresh - top)
            share = 1.0 / (
                jnp.sum(even + odd, axis=-1, keepdims=True)
                + jnp.sum(fresh, axis=-1, keepdims=True)
            )
            p_even.append((even * share).astype(jnp.bfloat16))
            p_odd.append((odd * share).astype(jnp.bfloat16))
            p_new.append((fresh * share).astype(jnp.bfloat16))
    p_even, p_odd, p_new = (jnp.concatenate(p, axis=0) for p in (p_even, p_odd, p_new))
    first = jnp.dot(p_even, k_even[:, :kv_rank], preferred_element_type=jnp.float32)
    second = jnp.dot(p_odd, k_odd[...], preferred_element_type=jnp.float32)
    third = jnp.dot(p_new, new[:, :kv_rank], preferred_element_type=jnp.float32)
    latent_out = (first + third + second[:, 64 : 64 + kv_rank]).astype(jnp.bfloat16)
    value_width = uv.shape[2]
    for h in range(head_here):
        heads[:, h * value_width : (h + 1) * value_width] = jnp.dot(
            latent_out[h * tok_rows : (h + 1) * tok_rows],
            uv[h],
            preferred_element_type=jnp.float32,
        )
    if sub_rows % 8:
        out[...] = heads[...].astype(jnp.bfloat16)
        return
    exp_index = place[1]
    blocks = []
    for m in order:
        for c in range(chunks):
            at = ((exp_index ^ m) * chunks + c) * sub_rows
            blocks.append(heads[pl.ds(pl.multiple_of(at, 8), sub_rows), :])
    out[...] = jnp.concatenate(blocks, axis=0).astype(jnp.bfloat16)


def local(
    queries,
    new_latent,
    pool,
    page_list,
    prefix_len,
    hidden_in,
    norm_gain,
    uv_weight,
    out_weight,
    route_ids,
    route_weight,
    gate_weight,
    up_weight,
    down_weight,
):
    req_count = lax.axis_size("req")
    exp_count = lax.axis_size("exp")
    req_index = lax.axis_index("req")
    exp_index = lax.axis_index("exp")
    tok_rows = queries.shape[0]
    latent = new_latent.shape[1]
    kv_rank = uv_weight.shape[1]
    value_width = uv_weight.shape[2]
    head_here = uv_weight.shape[0]
    pool_rows = pool.shape[0]
    page_size = pool.shape[1] // latent
    list_depth = page_list.shape[1]
    per_index = page_list.shape[0] // req_count
    depth_here = list_depth // req_count
    width = hidden_in.shape[1]
    col_width = width // req_count
    half_width = width // 2
    own_rows = tok_rows // exp_count
    sub_rows = own_rows // chunk_count
    outer = exp_count // 2
    req_rel = req_index ^ jnp.arange(req_count, dtype=jnp.int32)
    rel_order = [2 * k for k in range(outer)] + [2 * k + 1 for k in range(outer)]
    exp_rel = exp_index ^ jnp.array(rel_order, dtype=jnp.int32)

    slots = per_index * depth_here
    pair = 2 * latent
    pool_width = pool.shape[1]
    far_width = pool_width // exp_count
    far_split = min(16 // slots, far_width // pair)
    near_split = 16 // slots
    lengths = prefix_len.reshape(req_count, per_index)
    place = jnp.stack([req_index, exp_index]).astype(jnp.int32)
    plan = (
        req_count, per_index, depth_here, pool_rows, pool_width, far_width, far_split, near_split,
    )
    scalars = pl.BlockSpec(memory_space=pltpu.SMEM)
    whole = pl.BlockSpec(memory_space=pltpu.VMEM)
    far_shape = jax.ShapeDtypeStruct((16, far_width // far_split), jnp.bfloat16)
    sent = pl.pallas_call(
        functools.partial(pick_kernel, plan),
        out_shape=[far_shape] * (req_count - 1),
        in_specs=[scalars, scalars, whole],
        out_specs=[whole] * (req_count - 1),
        name="pick_far",
    )(place, page_list, pool)
    near = pl.pallas_call(
        functools.partial(near_kernel, plan),
        out_shape=jax.ShapeDtypeStruct((16, pool_width // near_split), jnp.bfloat16),
        in_specs=[scalars, scalars, whole],
        out_specs=whole,
        name="pick_near",
    )(place, page_list, pool)
    far = jnp.concatenate([swap(sent[j - 1], "req", j) for j in range(1, req_count)], axis=0)
    far_out = jnp.stack([far] + [swap(far, "exp", 2 * k) for k in range(1, outer)])
    far_all = jnp.concatenate([far_out, swap(far_out, "exp", 1)], axis=0)

    def positions(tokens, holder_ids, split, slot_row):
        depth = holder_ids * depth_here + slot_row % slots % depth_here
        return jnp.where(slot_row < slots * split, depth * page_size + tokens, list_depth * page_size)

    near_piece = page_size // near_split
    pairs = np.arange(near_piece // 2)[:, None]
    slot_row = np.arange(16)[None, :]
    near_pos = positions(slot_row // slots * near_piece + 2 * pairs, req_index, near_split, slot_row)
    near_req = np.broadcast_to(slot_row % slots // depth_here, near_pos.shape)
    far_tokens = page_size // exp_count
    far_piece = far_tokens // far_split
    pairs = np.arange(far_piece // 2).reshape(1, -1, 1, 1)
    slot_row = np.arange(16).reshape(1, 1, 1, -1)
    far_pos = positions(
        exp_rel.reshape(-1, 1, 1, 1) * far_tokens + slot_row // slots * far_piece + 2 * pairs,
        req_rel[1:].reshape(1, 1, -1, 1),
        far_split,
        slot_row,
    )
    far_req = np.broadcast_to(slot_row % slots // depth_here, far_pos.shape)
    key_pos = jnp.concatenate([near_pos.reshape(1, -1), far_pos.reshape(1, -1)], axis=1)
    key_req = np.concatenate([near_req.reshape(1, -1), far_req.reshape(1, -1)], axis=1)
    my_lengths = lax.dynamic_index_in_dim(lengths, req_index, 0, keepdims=False)[:, None]
    same = key_req == np.arange(per_index)[:, None]
    bias_even = jnp.where(same & (key_pos < my_lengths), 0.0, -1e30)
    bias_odd = jnp.where(same & (key_pos + 1 < my_lengths), 0.0, -1e30)
    new_count = tok_rows // per_index
    tok = np.arange(tok_rows)
    seen = (tok[:, None] // new_count == tok // new_count) & (tok <= tok[:, None])
    bias_new = jnp.asarray(np.where(seen, 0.0, -1e30), jnp.float32)
    by_head = queries.reshape(tok_rows, head_here, latent).transpose(1, 0, 2)
    by_head = by_head.reshape(head_here * tok_rows, latent)
    q_even = jnp.pad(by_head, ((0, 0), (0, 64)))
    q_odd = jnp.pad(by_head, ((0, 0), (64, 0)))
    new_keys = jnp.pad(new_latent, ((0, 0), (0, 64)))
    key_count = key_req.shape[1]
    q_rows = head_here * tok_rows
    head_cols = head_here * value_width
    head_out = pl.pallas_call(
        functools.partial(
            attention_kernel,
            (
                per_index, latent, kv_rank, head_here, tok_rows, tuple(rel_order), sub_rows,
                chunk_count,
            ),
        ),
        out_shape=jax.ShapeDtypeStruct((tok_rows, head_cols), jnp.bfloat16),
        in_specs=[scalars] + [whole] * 9,
        out_specs=whole,
        scratch_shapes=[
            pltpu.VMEM((key_count, latent + 64), jnp.bfloat16),
            pltpu.VMEM((key_count, latent + 64), jnp.bfloat16),
            pltpu.VMEM((q_rows, key_count), jnp.float32),
            pltpu.VMEM((q_rows, key_count), jnp.float32),
            pltpu.VMEM((tok_rows, head_cols), jnp.float32),
        ],
        compiler_params=pltpu.CompilerParams(vmem_limit_bytes=40 * 1024 * 1024),
        name="attention",
    )(place, near, far_all, new_keys, q_even, q_odd, bias_even, bias_odd, bias_new, uv_weight)
    head_out = head_out.reshape(exp_count, chunk_count, sub_rows, head_cols)
    if sub_rows % 8:
        head_out = head_out[exp_rel]

    chosen = route_ids == exp_index
    token_weight = jnp.sum(jnp.where(chosen, route_weight, 0.0), axis=1)
    token_weight = token_weight.reshape(exp_count, chunk_count, sub_rows)[exp_rel]
    weight_all = jnp.stack(
        [token_weight] + [swap(token_weight, "req", j) for j in range(1, req_count)]
    ).transpose(2, 1, 0, 3)

    hidden_cols = []
    for j in range(req_count):
        piece = lax.dynamic_slice_in_dim(hidden_in, req_rel[j] * col_width, col_width, 1)
        hidden_cols.append(piece if j == 0 else swap(piece, "req", j))
    hidden_cols = jnp.stack(hidden_cols).reshape(req_count, chunk_count, sub_rows, col_width)
    hidden_cols = hidden_cols.transpose(1, 0, 2, 3)

    heads_all = jnp.stack(
        [head_out] + [swap(head_out, "req", j) for j in range(1, req_count)], axis=2
    )
    block = req_count * sub_rows
    own_block = chunk_count * block
    partial = jnp.dot(
        heads_all.reshape(exp_count * own_block, head_cols),
        out_weight,
        preferred_element_type=jnp.float32,
    )
    cut = outer * own_block
    other = swap(partial[cut:].astype(jnp.bfloat16), "exp", 1)
    pair_sum = (partial[:cut] + other.astype(jnp.float32)).reshape(outer, own_block, col_width)
    attn = pair_sum[0]
    for k in range(1, outer):
        attn = attn + swap(pair_sum[k].astype(jnp.bfloat16), "exp", 2 * k).astype(jnp.float32)
    attn = attn.reshape(chunk_count, req_count, sub_rows, col_width)
    resid_cols = (hidden_cols.astype(jnp.float32) + attn).astype(jnp.bfloat16)

    def gather_columns(resid):
        slices = [resid]
        for j in range(1, req_count):
            got = swap(resid, "req", j)
            slices.append(jnp.stack([got[i ^ j] for i in range(req_count)]))
        ordered = jnp.stack(slices)[req_rel]
        return ordered.transpose(1, 2, 0, 3).reshape(block, width)

    def normalise(full):
        widened = full.astype(jnp.float32)
        inv_scale = lax.rsqrt(jnp.mean(widened * widened, axis=-1, keepdims=True) + norm_eps)
        return (widened * inv_scale * norm_gain.astype(jnp.float32)).astype(jnp.bfloat16)

    outer_bits = []
    bit = 1
    while bit < outer:
        outer_bits.append(bit)
        bit *= 2
    sides = (outer_bits, outer_bits[::-1])

    def gather_plane(piece, bits):
        held = piece[None]
        ids = [0]
        for bit in bits:
            held = jnp.concatenate([held, swap(held, "exp", 2 * bit)], axis=0)
            ids = ids + [k ^ bit for k in ids]
        back = [ids.index(k) for k in range(outer)]
        other = swap(held, "exp", 1)
        picks = [held[k] for k in back] + [other[k] for k in back]
        return jnp.concatenate(picks, axis=0)

    def scatter_plane(partial, bits):
        cut = outer * block
        other = swap(partial[cut:].astype(jnp.bfloat16), "exp", 1)
        held = (partial[:cut] + other.astype(jnp.float32)).reshape(outer, block, half_width)
        ids = list(range(outer))
        for bit in bits:
            keep = [n for n, k in enumerate(ids) if not k & bit]
            give = [ids.index(ids[n] ^ bit) for n in keep]
            sent = jnp.stack([held[n] for n in give]).astype(jnp.bfloat16)
            held = jnp.stack([held[n] for n in keep]) + swap(sent, "exp", 2 * bit).astype(
                jnp.float32
            )
            ids = [ids[n] for n in keep]
        return held[0].astype(jnp.bfloat16)

    gate_here = gate_weight[0]
    up_here = up_weight[0]
    down_here = down_weight[0]

    def experts(left, right, weights):
        def project(matrix):
            return jnp.dot(
                left, matrix[:half_width], preferred_element_type=jnp.float32
            ) + jnp.dot(right, matrix[half_width:], preferred_element_type=jnp.float32)

        active = (jax.nn.silu(project(gate_here)) * project(up_here)).astype(jnp.bfloat16)
        outs = []
        for matrix in (down_here[:, :half_width], down_here[:, half_width:]):
            out = jnp.dot(active, matrix, preferred_element_type=jnp.float32)
            outs.append(out * weights[:, None])
        return outs

    results = []
    for c in range(chunk_count):
        full = gather_columns(resid_cols[c])
        normed = normalise(full)
        rows = [
            gather_plane(normed[:, n * half_width : (n + 1) * half_width], sides[n])
            for n in range(2)
        ]
        outs = experts(rows[0], rows[1], weight_all[c].reshape(-1))
        sums = jnp.concatenate([scatter_plane(outs[n], sides[n]) for n in range(2)], axis=1)
        sums = sums.reshape(req_count, sub_rows, width)
        total = full[:sub_rows].astype(jnp.float32) + sums[0].astype(jnp.float32)
        for j in range(1, req_count):
            total = total + swap(sums[j], "req", j).astype(jnp.float32)
        results.append(total.astype(jnp.bfloat16))
    return jnp.concatenate(results, axis=0)


def solution(mesh):
    return jax.shard_map(
        local,
        mesh=mesh,
        in_specs=(
            P("req", "exp"),
            P("req", None),
            P("req", None),
            P(),
            P(),
            P(("req", "exp"), None),
            P(),
            P("exp", None, None),
            P("exp", "req"),
            P("req", None),
            P("req", None),
            P("exp", None, "req"),
            P("exp", None, "req"),
            P("exp", "req", None),
        ),
        out_specs=P(("req", "exp"), None),
        check_vma=False,
    )
```

```python
import functools

import jax
import jax.numpy as jnp
import numpy as np
from jax import lax
from jax.experimental import pallas as pl
from jax.experimental.pallas import tpu as pltpu
from jax.sharding import PartitionSpec as P

score_scale = 192.0 ** (-0.5)
norm_eps = 1e-06


def swap(x, axis, distance):
    size = lax.axis_size(axis)
    return lax.ppermute(x, axis, [(i, i ^ distance) for i in range(size)])


def after(x, *others):
    return lax.optimization_barrier((x,) + others)[0]


def pick_kernel(plan, place, lists, pool, *outs):
    req_count, per_index, depth_here, pool_rows, width, far_width, far_split, near_split = plan
    slots = per_index * depth_here
    req_index = place[0]
    row = lax.broadcasted_iota(jnp.int32, (16, pool_rows), 0)
    column = lax.broadcasted_iota(jnp.int32, (16, pool_rows), 1)

    def wanted(target):
        hot = row < 0
        for slot in range(slots):
            request, depth = slot // depth_here, slot % depth_here
            page = lists[target * per_index + request, req_index * depth_here + depth]
            hot = hot | ((row == slot) & (column == page - req_index * pool_rows))
        return hot.astype(jnp.float32)

    piece = far_width // far_split
    for out, j in zip(outs, range(1, req_count)):
        hot = wanted(req_index ^ j)
        total = jnp.zeros((16, piece), jnp.float32)
        for part in range(far_split):
            shifted = hot if part == 0 else pltpu.roll(hot, part * slots, 0)
            total = total + jnp.dot(
                shifted.astype(jnp.bfloat16),
                pool[:, part * piece : (part + 1) * piece],
                preferred_element_type=jnp.float32,
            )
        out[...] = total.astype(jnp.bfloat16)


def near_kernel(plan, place, lists, pool, out):
    req_count, per_index, depth_here, pool_rows, width, far_width, far_split, near_split = plan
    slots = per_index * depth_here
    req_index = place[0]
    row = lax.broadcasted_iota(jnp.int32, (16, pool_rows), 0)
    column = lax.broadcasted_iota(jnp.int32, (16, pool_rows), 1)
    hots = [row < 0] * near_split
    for slot in range(slots):
        request, depth = slot // depth_here, slot % depth_here
        page = lists[req_index * per_index + request, req_index * depth_here + depth]
        here = column == page - req_index * pool_rows
        for part in range(near_split):
            hots[part] = hots[part] | ((row == part * slots + slot) & here)
    hots = [hot.astype(jnp.float32).astype(jnp.bfloat16) for hot in hots]
    piece = width // near_split
    step = 1152
    for start in range(0, piece, step):
        total = jnp.zeros((16, step), jnp.float32)
        for part in range(near_split):
            cols = slice(part * piece + start, part * piece + start + step)
            total = total + jnp.dot(hots[part], pool[:, cols], preferred_element_type=jnp.float32)
        out[:, start : start + step] = total.astype(jnp.bfloat16)


def attention_kernel(
    plan, place, near, far, new, q_even, q_odd, bias_even, bias_odd, bias_new, uv, out,
    k_even, k_odd, s_even, s_odd, heads,
):
    per_index, latent, kv_rank, head_here, tok_rows, order, own_rows = plan
    pair = 2 * latent
    window = latent + 64
    lead = pair - window
    units, far_rows, far_width = far.shape
    near_rows = near.shape[0]
    base = 0

    def place_keys(rows, value_of, pairs, base):
        for p in range(pairs):
            k_even[base : base + rows, :] = value_of(p * pair, p * pair + window)
            k_odd[base : base + rows, :] = value_of(p * pair + lead, (p + 1) * pair)
            base += rows
        return base

    base = place_keys(near_rows, lambda a, b: near[:, a:b], near.shape[1] // pair, base)
    for m in range(units):
        base = place_keys(far_rows, lambda a, b: far[m, :, a:b], far_width // pair, base)
    rows_k = (((1,), (1,)), ((), ()))

    def times(a, b):
        return lax.dot_general(a, b, rows_k, preferred_element_type=jnp.float32) * score_scale

    s_even[...] = times(q_even[...], k_even[...])
    s_odd[...] = times(q_odd[...], k_odd[...])
    s_new = times(q_even[...], new[...])
    new_count = tok_rows // per_index
    p_even, p_odd, p_new = [], [], []
    for h in range(head_here):
        for i in range(per_index):
            at = h * tok_rows + i * new_count
            rows = slice(at, at + new_count)
            even = s_even[rows, :] + bias_even[i : i + 1, :]
            odd = s_odd[rows, :] + bias_odd[i : i + 1, :]
            fresh = s_new[rows, :] + bias_new[i * new_count : (i + 1) * new_count, :]
            top = jnp.maximum(
                jnp.max(jnp.maximum(even, odd), axis=-1, keepdims=True),
                jnp.max(fresh, axis=-1, keepdims=True),
            )
            even, odd, fresh = jnp.exp(even - top), jnp.exp(odd - top), jnp.exp(fresh - top)
            share = 1.0 / (
                jnp.sum(even + odd, axis=-1, keepdims=True)
                + jnp.sum(fresh, axis=-1, keepdims=True)
            )
            p_even.append((even * share).astype(jnp.bfloat16))
            p_odd.append((odd * share).astype(jnp.bfloat16))
            p_new.append((fresh * share).astype(jnp.bfloat16))
    p_even, p_odd, p_new = (jnp.concatenate(p, axis=0) for p in (p_even, p_odd, p_new))
    first = jnp.dot(p_even, k_even[:, :kv_rank], preferred_element_type=jnp.float32)
    second = jnp.dot(p_odd, k_odd[...], preferred_element_type=jnp.float32)
    third = jnp.dot(p_new, new[:, :kv_rank], preferred_element_type=jnp.float32)
    latent_out = (first + third + second[:, 64 : 64 + kv_rank]).astype(jnp.bfloat16)
    value_width = uv.shape[2]
    for h in range(head_here):
        heads[:, h * value_width : (h + 1) * value_width] = jnp.dot(
            latent_out[h * tok_rows : (h + 1) * tok_rows],
            uv[h],
            preferred_element_type=jnp.float32,
        )
    if own_rows % 8:
        out[...] = heads[...].astype(jnp.bfloat16)
        return
    exp_index = place[1]
    blocks = []
    for m in order:
        at = (exp_index ^ m) * own_rows
        blocks.append(heads[pl.ds(pl.multiple_of(at, 8), own_rows), :])
    out[...] = jnp.concatenate(blocks, axis=0).astype(jnp.bfloat16)


def local(
    queries,
    new_latent,
    pool,
    page_list,
    prefix_len,
    hidden_in,
    norm_gain,
    uv_weight,
    out_weight,
    route_ids,
    route_weight,
    gate_weight,
    up_weight,
    down_weight,
):
    req_count = lax.axis_size("req")
    exp_count = lax.axis_size("exp")
    req_index = lax.axis_index("req")
    exp_index = lax.axis_index("exp")
    tok_rows = queries.shape[0]
    latent = new_latent.shape[1]
    kv_rank = uv_weight.shape[1]
    value_width = uv_weight.shape[2]
    head_here = uv_weight.shape[0]
    pool_rows = pool.shape[0]
    page_size = pool.shape[1] // latent
    list_depth = page_list.shape[1]
    per_index = page_list.shape[0] // req_count
    depth_here = list_depth // req_count
    width = hidden_in.shape[1]
    col_width = width // req_count
    half_width = width // 2
    own_rows = tok_rows // exp_count
    outer = exp_count // 2
    req_rel = req_index ^ jnp.arange(req_count, dtype=jnp.int32)
    rel_order = [2 * k for k in range(outer)] + [2 * k + 1 for k in range(outer)]
    exp_rel = exp_index ^ jnp.array(rel_order, dtype=jnp.int32)

    slots = per_index * depth_here
    pair = 2 * latent
    pool_width = pool.shape[1]
    far_width = pool_width // exp_count
    far_split = min(16 // slots, far_width // pair)
    near_split = 16 // slots
    lengths = prefix_len.reshape(req_count, per_index)
    place = jnp.stack([req_index, exp_index]).astype(jnp.int32)
    plan = (
        req_count, per_index, depth_here, pool_rows, pool_width, far_width, far_split, near_split,
    )
    scalars = pl.BlockSpec(memory_space=pltpu.SMEM)
    whole = pl.BlockSpec(memory_space=pltpu.VMEM)
    far_shape = jax.ShapeDtypeStruct((16, far_width // far_split), jnp.bfloat16)
    sent = pl.pallas_call(
        functools.partial(pick_kernel, plan),
        out_shape=[far_shape] * (req_count - 1),
        grid_spec=pltpu.PrefetchScalarGridSpec(
            num_scalar_prefetch=2,
            grid=(1,),
            in_specs=[pl.BlockSpec((pool_rows, far_width), lambda n, place, lists: (0, place[1]))],
            out_specs=[whole] * (req_count - 1),
        ),
        name="pick_far",
    )(place, page_list, pool)
    near = pl.pallas_call(
        functools.partial(near_kernel, plan),
        out_shape=jax.ShapeDtypeStruct((16, pool_width // near_split), jnp.bfloat16),
        in_specs=[scalars, scalars, whole],
        out_specs=whole,
        name="pick_near",
    )(place, page_list, pool)
    far = jnp.concatenate([swap(sent[j - 1], "req", j) for j in range(1, req_count)], axis=0)
    far_out = jnp.stack([far] + [swap(far, "exp", 2 * k) for k in range(1, outer)])
    far_all = jnp.concatenate([far_out, swap(far_out, "exp", 1)], axis=0)

    def positions(tokens, holder_ids, split, slot_row):
        depth = holder_ids * depth_here + slot_row % slots % depth_here
        return jnp.where(slot_row < slots * split, depth * page_size + tokens, list_depth * page_size)

    chosen = route_ids == exp_index
    token_weight = jnp.sum(jnp.where(chosen, route_weight, 0.0), axis=1)
    token_weight = token_weight.reshape(exp_count, own_rows)[exp_rel]
    behind = [after(token_weight, far)] * (req_count - 1)
    weight_all = jnp.stack(
        [token_weight] + [swap(behind[j - 1], "req", j) for j in range(1, req_count)], axis=1
    )
    hidden_cols = []
    for j in range(req_count):
        piece = lax.dynamic_slice_in_dim(hidden_in, req_rel[j] * col_width, col_width, 1)
        hidden_cols.append(piece if j == 0 else swap(after(piece, far), "req", j))
    hidden_cols = jnp.concatenate(hidden_cols, axis=0)
    near, hidden_cols, weight_all = lax.optimization_barrier((near, hidden_cols, weight_all))

    near_piece = page_size // near_split
    pairs = np.arange(near_piece // 2)[:, None]
    slot_row = np.arange(16)[None, :]
    near_pos = positions(slot_row // slots * near_piece + 2 * pairs, req_index, near_split, slot_row)
    near_req = np.broadcast_to(slot_row % slots // depth_here, near_pos.shape)
    far_tokens = page_size // exp_count
    far_piece = far_tokens // far_split
    pairs = np.arange(far_piece // 2).reshape(1, -1, 1, 1)
    slot_row = np.arange(16).reshape(1, 1, 1, -1)
    far_pos = positions(
        exp_rel.reshape(-1, 1, 1, 1) * far_tokens + slot_row // slots * far_piece + 2 * pairs,
        req_rel[1:].reshape(1, 1, -1, 1),
        far_split,
        slot_row,
    )
    far_req = np.broadcast_to(slot_row % slots // depth_here, far_pos.shape)
    key_pos = jnp.concatenate([near_pos.reshape(1, -1), far_pos.reshape(1, -1)], axis=1)
    key_req = np.concatenate([near_req.reshape(1, -1), far_req.reshape(1, -1)], axis=1)
    my_lengths = lax.dynamic_index_in_dim(lengths, req_index, 0, keepdims=False)[:, None]
    same = key_req == np.arange(per_index)[:, None]
    bias_even = jnp.where(same & (key_pos < my_lengths), 0.0, -1e30)
    bias_odd = jnp.where(same & (key_pos + 1 < my_lengths), 0.0, -1e30)
    new_count = tok_rows // per_index
    tok = np.arange(tok_rows)
    seen = (tok[:, None] // new_count == tok // new_count) & (tok <= tok[:, None])
    bias_new = jnp.asarray(np.where(seen, 0.0, -1e30), jnp.float32)
    by_head = queries.reshape(tok_rows, head_here, latent).transpose(1, 0, 2)
    by_head = by_head.reshape(head_here * tok_rows, latent)
    q_even = jnp.pad(by_head, ((0, 0), (0, 64)))
    q_odd = jnp.pad(by_head, ((0, 0), (64, 0)))
    new_keys = jnp.pad(new_latent, ((0, 0), (0, 64)))
    key_count = key_req.shape[1]
    q_rows = head_here * tok_rows
    head_cols = head_here * value_width
    head_out = pl.pallas_call(
        functools.partial(
            attention_kernel,
            (
                per_index, latent, kv_rank, head_here, tok_rows, tuple(rel_order), own_rows,
            ),
        ),
        out_shape=jax.ShapeDtypeStruct((tok_rows, head_cols), jnp.bfloat16),
        in_specs=[scalars] + [whole] * 9,
        out_specs=whole,
        scratch_shapes=[
            pltpu.VMEM((key_count, latent + 64), jnp.bfloat16),
            pltpu.VMEM((key_count, latent + 64), jnp.bfloat16),
            pltpu.VMEM((q_rows, key_count), jnp.float32),
            pltpu.VMEM((q_rows, key_count), jnp.float32),
            pltpu.VMEM((tok_rows, head_cols), jnp.float32),
        ],
        compiler_params=pltpu.CompilerParams(vmem_limit_bytes=40 * 1024 * 1024),
        name="attention",
    )(place, near, far_all, new_keys, q_even, q_odd, bias_even, bias_odd, bias_new, uv_weight)
    head_out = head_out.reshape(exp_count, own_rows, head_cols)
    if own_rows % 8:
        head_out = head_out[exp_rel]

    heads_all = jnp.stack(
        [head_out] + [swap(head_out, "req", j) for j in range(1, req_count)], axis=1
    )
    block = req_count * own_rows
    partial = jnp.dot(
        heads_all.reshape(exp_count * block, head_cols),
        out_weight,
        preferred_element_type=jnp.float32,
    )
    cut = outer * block
    other = swap(partial[cut:].astype(jnp.bfloat16), "exp", 1)
    pair_sum = (partial[:cut] + other.astype(jnp.float32)).reshape(outer, block, col_width)
    attn = pair_sum[0]
    for k in range(1, outer):
        attn = attn + swap(pair_sum[k].astype(jnp.bfloat16), "exp", 2 * k).astype(jnp.float32)
    resid = (hidden_cols.astype(jnp.float32) + attn).astype(jnp.bfloat16)

    pieces = [resid]
    for b in range(1, req_count):
        got = swap(resid if b < 3 else after(resid, pieces[b - 2]), "req", b)
        got = got.reshape(req_count, own_rows, col_width)
        pieces.append(jnp.concatenate([got[i ^ b] for i in range(req_count)], axis=0))

    outer_bits = []
    bit = 1
    while bit < outer:
        outer_bits.append(bit)
        bit *= 2
    orders = (outer_bits, outer_bits[::-1])

    def gather_side(piece, bits):
        held = piece[None]
        ids = [0]
        for bit in bits:
            held = jnp.concatenate([held, swap(held, "exp", 2 * bit)], axis=0)
            ids = ids + [k ^ bit for k in ids]
        return [held[ids.index(k)] for k in range(outer)]

    def gather_plane(piece):
        half = piece.shape[0] // 2
        first = gather_side(piece[:half], orders[0])
        second = gather_side(piece[half:], orders[1])
        same = jnp.concatenate([p for pair in zip(first, second) for p in pair], axis=0)
        return jnp.concatenate([same, swap(same, "exp", 1)], axis=0)

    gate_here = gate_weight[0]
    up_here = up_weight[0]
    down_here = down_weight[0]
    gain = norm_gain.astype(jnp.float32)
    gate_val = up_val = squares = 0.0
    span = max(1, req_count // 4)
    slices = []
    for b in range(0, req_count, span):
        rows = gather_plane(jnp.concatenate(pieces[b : b + span], axis=0))
        rows = rows.reshape(exp_count, span, block, col_width)
        slices += [rows[:, n].reshape(exp_count * block, col_width) for n in range(span)]
    for b in range(req_count):
        start = req_rel[b] * col_width
        rows = slices[b].astype(jnp.float32)
        squares = squares + jnp.sum(rows * rows, axis=-1, keepdims=True)
        scaled = (rows * lax.dynamic_slice_in_dim(gain, start, col_width)).astype(jnp.bfloat16)
        gate_val = gate_val + jnp.dot(
            scaled,
            lax.dynamic_slice_in_dim(gate_here, start, col_width),
            preferred_element_type=jnp.float32,
        )
        up_val = up_val + jnp.dot(
            scaled,
            lax.dynamic_slice_in_dim(up_here, start, col_width),
            preferred_element_type=jnp.float32,
        )
    inv_scale = lax.rsqrt(squares / width + norm_eps)
    active = (jax.nn.silu(gate_val * inv_scale) * (up_val * inv_scale)).astype(jnp.bfloat16)
    active = active.reshape(exp_count, req_count, own_rows, -1)

    def scatter_side(held, bits):
        ids = list(range(outer))
        for bit in bits:
            keep = [n for n, k in enumerate(ids) if not k & bit]
            give = [ids.index(ids[n] ^ bit) for n in keep]
            sent = jnp.stack([held[n] for n in give]).astype(jnp.bfloat16)
            held = jnp.stack([held[n] for n in keep]) + swap(sent, "exp", 2 * bit).astype(
                jnp.float32
            )
            ids = [ids[n] for n in keep]
        return held[0].astype(jnp.bfloat16)

    own = jnp.stack([piece[:own_rows] for piece in pieces])[req_rel]
    total = own.transpose(1, 0, 2).reshape(own_rows, width).astype(jnp.float32)
    previous = None
    for j in reversed(range(0, req_count, span)):
        rows = active[:, j : j + span].reshape(span * tok_rows, -1)
        if previous is not None:
            rows = after(rows, previous)
        out = jnp.dot(rows, down_here, preferred_element_type=jnp.float32)
        out = out * weight_all[:, j : j + span].reshape(span * tok_rows, 1)
        cut = span * tok_rows // 2
        previous = out[cut:].astype(jnp.bfloat16)
        pair_sum = out[:cut] + swap(previous, "exp", 1).astype(jnp.float32)
        pair_sum = pair_sum.reshape(outer, span * own_rows, width)
        sums = [
            scatter_side(pair_sum[:, :, :half_width], orders[0]),
            scatter_side(pair_sum[:, :, half_width:], orders[1]),
        ]
        sums = jnp.concatenate(sums, axis=1)
        for n in reversed(range(span)):
            part = sums[n * own_rows : (n + 1) * own_rows]
            part = swap(part, "req", j + n) if j + n else part
            total = total + part.astype(jnp.float32)
    return total.astype(jnp.bfloat16)


def solution(mesh):
    return jax.shard_map(
        local,
        mesh=mesh,
        in_specs=(
            P("req", "exp"),
            P("req", None),
            P("req", None),
            P(),
            P(),
            P(("req", "exp"), None),
            P(),
            P("exp", None, None),
            P("exp", "req"),
            P("req", None),
            P("req", None),
            P("exp", None, "req"),
            P("exp", None, "req"),
            P("exp", "req", None),
        ),
        out_specs=P(("req", "exp"), None),
        check_vma=False,
    )
```

```python
import functools

import jax
import jax.numpy as jnp
import numpy as np
from jax import lax
from jax.experimental import pallas as pl
from jax.experimental.pallas import tpu as pltpu
from jax.sharding import PartitionSpec as P

score_scale = 192.0 ** (-0.5)
norm_eps = 1e-06


def swap(x, axis, distance):
    size = lax.axis_size(axis)
    return lax.ppermute(x, axis, [(i, i ^ distance) for i in range(size)])


def pick_kernel(plan, place, lists, pool, *outs):
    req_count, per_index, depth_here, pool_rows, width, far_width, far_split, near_split = plan
    slots = per_index * depth_here
    req_index = place[0]
    row = lax.broadcasted_iota(jnp.int32, (16, pool_rows), 0)
    column = lax.broadcasted_iota(jnp.int32, (16, pool_rows), 1)

    def wanted(target):
        hot = row < 0
        for slot in range(slots):
            request, depth = slot // depth_here, slot % depth_here
            page = lists[target * per_index + request, req_index * depth_here + depth]
            hot = hot | ((row == slot) & (column == page - req_index * pool_rows))
        return hot.astype(jnp.float32)

    piece = far_width // far_split
    for out, j in zip(outs, range(1, req_count)):
        hot = wanted(req_index ^ j)
        total = jnp.zeros((16, piece), jnp.float32)
        for part in range(far_split):
            shifted = hot if part == 0 else pltpu.roll(hot, part * slots, 0)
            total = total + jnp.dot(
                shifted.astype(jnp.bfloat16),
                pool[:, part * piece : (part + 1) * piece],
                preferred_element_type=jnp.float32,
            )
        out[...] = total.astype(jnp.bfloat16)


def near_kernel(plan, place, lists, pool, out):
    req_count, per_index, depth_here, pool_rows, width, far_width, far_split, near_split = plan
    slots = per_index * depth_here
    req_index = place[0]
    row = lax.broadcasted_iota(jnp.int32, (16, pool_rows), 0)
    column = lax.broadcasted_iota(jnp.int32, (16, pool_rows), 1)
    hots = [row < 0] * near_split
    for slot in range(slots):
        request, depth = slot // depth_here, slot % depth_here
        page = lists[req_index * per_index + request, req_index * depth_here + depth]
        here = column == page - req_index * pool_rows
        for part in range(near_split):
            hots[part] = hots[part] | ((row == part * slots + slot) & here)
    hots = [hot.astype(jnp.float32).astype(jnp.bfloat16) for hot in hots]
    piece = width // near_split
    step = 1152
    for start in range(0, piece, step):
        total = jnp.zeros((16, step), jnp.float32)
        for part in range(near_split):
            cols = slice(part * piece + start, part * piece + start + step)
            total = total + jnp.dot(hots[part], pool[:, cols], preferred_element_type=jnp.float32)
        out[:, start : start + step] = total.astype(jnp.bfloat16)


def attention_kernel(
    plan, place, near, far, new, q_even, q_odd, bias_even, bias_odd, bias_new, uv, extra, out,
    k_even, k_odd, s_even, s_odd, heads,
):
    per_index, latent, kv_rank, head_here, tok_rows, order, own_rows = plan
    pair = 2 * latent
    window = latent + 64
    lead = pair - window
    units, far_rows, far_width = far.shape
    near_rows = near.shape[0]
    base = 0

    def place_keys(rows, value_of, pairs, base):
        for p in range(pairs):
            k_even[base : base + rows, :] = value_of(p * pair, p * pair + window)
            k_odd[base : base + rows, :] = value_of(p * pair + lead, (p + 1) * pair)
            base += rows
        return base

    base = place_keys(near_rows, lambda a, b: near[:, a:b], near.shape[1] // pair, base)
    for m in range(units):
        base = place_keys(far_rows, lambda a, b: far[m, :, a:b], far_width // pair, base)
    rows_k = (((1,), (1,)), ((), ()))

    def times(a, b):
        return lax.dot_general(a, b, rows_k, preferred_element_type=jnp.float32) * score_scale

    s_even[...] = times(q_even[...], k_even[...])
    s_odd[...] = times(q_odd[...], k_odd[...])
    s_new = times(q_even[...], new[...])
    new_count = tok_rows // per_index
    p_even, p_odd, p_new = [], [], []
    for h in range(head_here):
        for i in range(per_index):
            at = h * tok_rows + i * new_count
            rows = slice(at, at + new_count)
            even = s_even[rows, :] + bias_even[i : i + 1, :]
            odd = s_odd[rows, :] + bias_odd[i : i + 1, :]
            fresh = s_new[rows, :] + bias_new[i * new_count : (i + 1) * new_count, :]
            top = jnp.maximum(
                jnp.max(jnp.maximum(even, odd), axis=-1, keepdims=True),
                jnp.max(fresh, axis=-1, keepdims=True),
            )
            even, odd, fresh = jnp.exp(even - top), jnp.exp(odd - top), jnp.exp(fresh - top)
            share = 1.0 / (
                jnp.sum(even + odd, axis=-1, keepdims=True)
                + jnp.sum(fresh, axis=-1, keepdims=True)
            )
            p_even.append((even * share).astype(jnp.bfloat16))
            p_odd.append((odd * share).astype(jnp.bfloat16))
            p_new.append((fresh * share).astype(jnp.bfloat16))
    p_even, p_odd, p_new = (jnp.concatenate(p, axis=0) for p in (p_even, p_odd, p_new))
    first = jnp.dot(p_even, k_even[:, :kv_rank], preferred_element_type=jnp.float32)
    second = jnp.dot(p_odd, k_odd[...], preferred_element_type=jnp.float32)
    third = jnp.dot(p_new, new[:, :kv_rank], preferred_element_type=jnp.float32)
    latent_out = (first + third + second[:, 64 : 64 + kv_rank]).astype(jnp.bfloat16)
    value_width = uv.shape[2]
    for h in range(head_here):
        heads[:, h * value_width : (h + 1) * value_width] = jnp.dot(
            latent_out[h * tok_rows : (h + 1) * tok_rows],
            uv[h],
            preferred_element_type=jnp.float32,
        )
    out[tok_rows:, :] = extra[...]
    if own_rows % 8:
        out[:tok_rows, :] = heads[...].astype(jnp.bfloat16)
        return
    exp_index = place[1]
    blocks = []
    for m in order:
        at = (exp_index ^ m) * own_rows
        blocks.append(heads[pl.ds(pl.multiple_of(at, 8), own_rows), :])
    out[:tok_rows, :] = jnp.concatenate(blocks, axis=0).astype(jnp.bfloat16)


def hold_kernel(x, other, out):
    del other
    out[...] = x[...]


def collect_kernel(*refs):
    out, base = refs[-1], 0
    for ref in refs[:-2]:
        out[base : base + ref.shape[0], :] = ref[...]
        base += ref.shape[0]


def multiply_kernel(plan, place, same, other, gain, gate, up, *refs):
    shift, req_count, own_rows, width, first, last = plan
    old, refs = (None, refs) if first else (refs[:3], refs[3:])
    outs, (scaled, sums) = refs[:-2], refs[-2:]
    rows, columns = same.shape
    start = pl.multiple_of((place[0] ^ shift) * columns, 128)
    gains = gain[:, pl.ds(start, columns)]
    unit = own_rows if own_rows % 16 == 0 else req_count * own_rows
    for half, ref in enumerate((same, other)):
        for n in range(rows // unit):
            to = n if unit > own_rows else n ^ shift
            at = half * rows + to * unit
            block = ref[n * unit : (n + 1) * unit, :].astype(jnp.float32)
            scaled[at : at + unit, :] = (block * gains).astype(jnp.bfloat16)
            block = block * block
            total = block[:, :128]
            for c in range(128, columns, 128):
                total = total + block[:, c : c + 128]
            sums[at : at + unit, :] = total
    if first:
        squares = sums[...]
    else:
        squares = old[2][...] + sums[...]
    if last:
        mean = jnp.sum(squares, axis=-1, keepdims=True) / width
        inv_scale = lax.rsqrt(mean + norm_eps)
    else:
        outs[2][...] = squares
    tile = min(256, gate.shape[1])
    for n in range(0, gate.shape[1], tile):
        cols = slice(n, n + tile)
        values = []
        for k, weight in enumerate((gate, up)):
            value = jnp.dot(
                scaled[...], weight[pl.ds(start, columns), cols], preferred_element_type=jnp.float32
            )
            values.append(value if first else value + old[k][:, cols])
        if last:
            gate_val, up_val = (value * inv_scale for value in values)
            active = gate_val / (1.0 + jnp.exp(-gate_val)) * up_val
            outs[0][:, cols] = active.astype(jnp.bfloat16)
        else:
            outs[0][:, cols] = values[0]
            outs[1][:, cols] = values[1]


def down_kernel(rows, down, weights, other, give, keep):
    del other
    half = keep.shape[0]
    tile = 512

    def step(n, carry):
        cols = pl.ds(pl.multiple_of(n * tile, tile), tile)
        out = jnp.dot(rows[...], down[:, cols], preferred_element_type=jnp.float32)
        out = out * weights[...]
        keep[:, cols] = out[:half]
        give[:, cols] = out[half:].astype(jnp.bfloat16)
        return carry

    lax.fori_loop(0, down.shape[1] // tile, step, 0)


def local(
    queries,
    new_latent,
    pool,
    page_list,
    prefix_len,
    hidden_in,
    norm_gain,
    uv_weight,
    out_weight,
    route_ids,
    route_weight,
    gate_weight,
    up_weight,
    down_weight,
):
    req_count = lax.axis_size("req")
    exp_count = lax.axis_size("exp")
    req_index = lax.axis_index("req")
    exp_index = lax.axis_index("exp")
    tok_rows = queries.shape[0]
    latent = new_latent.shape[1]
    kv_rank = uv_weight.shape[1]
    value_width = uv_weight.shape[2]
    head_here = uv_weight.shape[0]
    pool_rows = pool.shape[0]
    page_size = pool.shape[1] // latent
    list_depth = page_list.shape[1]
    per_index = page_list.shape[0] // req_count
    depth_here = list_depth // req_count
    width = hidden_in.shape[1]
    col_width = width // req_count
    half_width = width // 2
    own_rows = tok_rows // exp_count
    outer = exp_count // 2
    req_rel = req_index ^ jnp.arange(req_count, dtype=jnp.int32)
    rel_order = [2 * k for k in range(outer)] + [2 * k + 1 for k in range(outer)]
    exp_rel = exp_index ^ jnp.array(rel_order, dtype=jnp.int32)

    slots = per_index * depth_here
    pair = 2 * latent
    pool_width = pool.shape[1]
    far_width = pool_width // exp_count
    far_split = min(16 // slots, far_width // pair)
    near_split = 16 // slots
    lengths = prefix_len.reshape(req_count, per_index)
    place = jnp.stack([req_index, exp_index]).astype(jnp.int32)
    plan = (
        req_count, per_index, depth_here, pool_rows, pool_width, far_width, far_split, near_split,
    )
    scalars = pl.BlockSpec(memory_space=pltpu.SMEM)
    whole = pl.BlockSpec(memory_space=pltpu.VMEM)
    far_shape = jax.ShapeDtypeStruct((16, far_width // far_split), jnp.bfloat16)
    sent = pl.pallas_call(
        functools.partial(pick_kernel, plan),
        out_shape=[far_shape] * (req_count - 1),
        grid_spec=pltpu.PrefetchScalarGridSpec(
            num_scalar_prefetch=2,
            grid=(1,),
            in_specs=[pl.BlockSpec((pool_rows, far_width), lambda n, place, lists: (0, place[1]))],
            out_specs=[whole] * (req_count - 1),
        ),
        name="pick_far",
    )(place, page_list, pool)
    near = pl.pallas_call(
        functools.partial(near_kernel, plan),
        out_shape=jax.ShapeDtypeStruct((16, pool_width // near_split), jnp.bfloat16),
        in_specs=[scalars, scalars, whole],
        out_specs=whole,
        name="pick_near",
    )(place, page_list, pool)
    far = jnp.concatenate([swap(sent[j - 1], "req", j) for j in range(1, req_count)], axis=0)
    far_out = jnp.stack([far] + [swap(far, "exp", 2 * k) for k in range(1, outer)])
    far_all = jnp.concatenate([far_out, swap(far_out, "exp", 1)], axis=0)

    def positions(tokens, holder_ids, split, slot_row):
        depth = holder_ids * depth_here + slot_row % slots % depth_here
        return jnp.where(slot_row < slots * split, depth * page_size + tokens, list_depth * page_size)

    chosen = route_ids == exp_index
    token_weight = jnp.sum(jnp.where(chosen, route_weight, 0.0), axis=1)
    token_weight = token_weight.reshape(exp_count, own_rows)[exp_rel].reshape(-1)
    parts, left = [], token_weight
    for n in range(3):
        part = lax.reduce_precision(left, 8, 7)
        left = left - part
        parts.append(part.astype(jnp.bfloat16))
    head_cols = head_here * value_width
    extra_rows = -(-3 * tok_rows // (16 * head_cols)) * 16
    extra = jnp.concatenate(parts)
    extra = jnp.pad(extra, (0, extra_rows * head_cols - 3 * tok_rows))
    extra = extra.reshape(extra_rows, head_cols)

    hidden_cols = []
    for j in range(req_count):
        piece = lax.dynamic_slice_in_dim(hidden_in, req_rel[j] * col_width, col_width, 1)
        hidden_cols.append(piece if j == 0 else swap(piece, "req", j))
    hidden_cols = jnp.concatenate(hidden_cols, axis=0)

    near_piece = page_size // near_split
    pairs = np.arange(near_piece // 2)[:, None]
    slot_row = np.arange(16)[None, :]
    near_pos = positions(slot_row // slots * near_piece + 2 * pairs, req_index, near_split, slot_row)
    near_req = np.broadcast_to(slot_row % slots // depth_here, near_pos.shape)
    far_tokens = page_size // exp_count
    far_piece = far_tokens // far_split
    pairs = np.arange(far_piece // 2).reshape(1, -1, 1, 1)
    slot_row = np.arange(16).reshape(1, 1, 1, -1)
    far_pos = positions(
        exp_rel.reshape(-1, 1, 1, 1) * far_tokens + slot_row // slots * far_piece + 2 * pairs,
        req_rel[1:].reshape(1, 1, -1, 1),
        far_split,
        slot_row,
    )
    far_req = np.broadcast_to(slot_row % slots // depth_here, far_pos.shape)
    key_pos = jnp.concatenate([near_pos.reshape(1, -1), far_pos.reshape(1, -1)], axis=1)
    key_req = np.concatenate([near_req.reshape(1, -1), far_req.reshape(1, -1)], axis=1)
    my_lengths = lax.dynamic_index_in_dim(lengths, req_index, 0, keepdims=False)[:, None]
    same = key_req == np.arange(per_index)[:, None]
    bias_even = jnp.where(same & (key_pos < my_lengths), 0.0, -1e30)
    bias_odd = jnp.where(same & (key_pos + 1 < my_lengths), 0.0, -1e30)
    new_count = tok_rows // per_index
    tok = np.arange(tok_rows)
    seen = (tok[:, None] // new_count == tok // new_count) & (tok <= tok[:, None])
    bias_new = jnp.asarray(np.where(seen, 0.0, -1e30), jnp.float32)
    by_head = queries.reshape(tok_rows, head_here, latent).transpose(1, 0, 2)
    by_head = by_head.reshape(head_here * tok_rows, latent)
    q_even = jnp.pad(by_head, ((0, 0), (0, 64)))
    q_odd = jnp.pad(by_head, ((0, 0), (64, 0)))
    new_keys = jnp.pad(new_latent, ((0, 0), (0, 64)))
    key_count = key_req.shape[1]
    q_rows = head_here * tok_rows
    head_out = pl.pallas_call(
        functools.partial(
            attention_kernel,
            (
                per_index, latent, kv_rank, head_here, tok_rows, tuple(rel_order), own_rows,
            ),
        ),
        out_shape=jax.ShapeDtypeStruct((tok_rows + extra_rows, head_cols), jnp.bfloat16),
        in_specs=[scalars] + [whole] * 10,
        out_specs=whole,
        scratch_shapes=[
            pltpu.VMEM((key_count, latent + 64), jnp.bfloat16),
            pltpu.VMEM((key_count, latent + 64), jnp.bfloat16),
            pltpu.VMEM((q_rows, key_count), jnp.float32),
            pltpu.VMEM((q_rows, key_count), jnp.float32),
            pltpu.VMEM((tok_rows, head_cols), jnp.float32),
        ],
        compiler_params=pltpu.CompilerParams(vmem_limit_bytes=40 * 1024 * 1024),
        name="attention",
    )(place, near, far_all, new_keys, q_even, q_odd, bias_even, bias_odd, bias_new, uv_weight, extra)
    if own_rows % 8:
        ordered = head_out[:tok_rows].reshape(exp_count, own_rows, head_cols)[exp_rel]
        head_out = jnp.concatenate([ordered.reshape(tok_rows, head_cols), head_out[tok_rows:]])

    heads = [head_out] + [swap(head_out, "req", j) for j in range(1, req_count)]
    heads_all = jnp.stack(
        [h[:tok_rows].reshape(exp_count, own_rows, head_cols) for h in heads], axis=1
    )
    weight_all = jnp.stack([h[tok_rows:].reshape(-1)[: 3 * tok_rows] for h in heads])
    weight_all = weight_all.astype(jnp.float32).reshape(req_count, 3, exp_count, own_rows)
    weight_all = (weight_all[:, 0] + weight_all[:, 1] + weight_all[:, 2]).transpose(1, 0, 2)
    block = req_count * own_rows
    partial = jnp.dot(
        heads_all.reshape(exp_count * block, head_cols),
        out_weight,
        preferred_element_type=jnp.float32,
    )
    cut = outer * block
    other = swap(partial[cut:].astype(jnp.bfloat16), "exp", 1)
    pair_sum = (partial[:cut] + other.astype(jnp.float32)).reshape(outer, block, col_width)
    attn = pair_sum[0]
    for k in range(1, outer):
        attn = attn + swap(pair_sum[k].astype(jnp.bfloat16), "exp", 2 * k).astype(jnp.float32)
    resid = (hidden_cols.astype(jnp.float32) + attn).astype(jnp.bfloat16)

    outer_bits = []
    bit = 1
    while bit < outer:
        outer_bits.append(bit)
        bit *= 2
    somewhere = pl.BlockSpec(memory_space=pl.ANY)

    def hold(x, other):
        return pl.pallas_call(
            hold_kernel,
            out_shape=jax.ShapeDtypeStruct(x.shape, x.dtype),
            in_specs=[whole, somewhere],
            out_specs=whole,
            name="hold",
        )(x, other)

    def collect(blocks, other):
        rows = sum(x.shape[0] for x in blocks)
        return pl.pallas_call(
            collect_kernel,
            out_shape=jax.ShapeDtypeStruct((rows, blocks[0].shape[1]), blocks[0].dtype),
            in_specs=[whole] * len(blocks) + [somewhere],
            out_specs=whole,
            name="collect",
        )(*blocks, other)

    def gather_outer(piece):
        if outer == 4:
            half = piece.shape[0] // 2
            along_x, along_y = swap(piece, "exp", 2), swap(piece, "exp", 4)
            near_half = swap(along_x[:half], "exp", 4)
            far_half = swap(along_y[half:], "exp", 2)
            return [piece, along_x, along_y, near_half, far_half]
        held = piece[None]
        for bit in outer_bits:
            held = jnp.concatenate([held, swap(held, "exp", 2 * bit)], axis=0)
        return list(held)

    def scatter_outer(held):
        if outer == 4:
            half = held.shape[2] // 2
            from_x = swap(held[3, :, :half].astype(jnp.bfloat16), "exp", 2)
            from_y = swap(held[3, :, half:].astype(jnp.bfloat16), "exp", 4)
            to_x = jnp.concatenate([held[1, :, :half], held[1, :, half:] + from_y], axis=1)
            to_y = jnp.concatenate([held[2, :, :half] + from_x, held[2, :, half:]], axis=1)
            return (
                held[0]
                + swap(to_x.astype(jnp.bfloat16), "exp", 2)
                + swap(to_y.astype(jnp.bfloat16), "exp", 4)
            )
        for bit in reversed(outer_bits):
            sent = swap(held[bit:].astype(jnp.bfloat16), "exp", 2 * bit)
            held = held[:bit] + sent.astype(jnp.float32)
        return held[0]

    pieces = [resid]
    for b in range(1, req_count):
        pieces.append(swap(resid if b < 3 else hold(resid, pieces[b - 2]), "req", b))
    aligned = own_rows % 16 == 0
    if not aligned:
        for b in range(1, req_count):
            got = pieces[b].reshape(req_count, own_rows, col_width)
            pieces[b] = jnp.concatenate([got[i ^ b] for i in range(req_count)], axis=0)
    span = max(1, req_count // 4)
    ffe = gate_weight.shape[2]
    rows_all = exp_count * block
    gain = norm_gain.astype(jnp.float32).reshape(1, width)
    sum_shape = jax.ShapeDtypeStruct((rows_all, ffe), jnp.float32)
    square_shape = jax.ShapeDtypeStruct((rows_all, 128), jnp.float32)
    carry = []
    for b in range(0, req_count, span):
        piece = jnp.concatenate(pieces[b : b + span], axis=0)
        same = collect(gather_outer(piece), carry[0] if carry else extra)
        other = swap(same, "exp", 1)
        for n in range(span):
            first, last = b + n == 0, b + n == req_count - 1
            plan = (b + n, req_count, own_rows, width, first, last)
            pair_rows = [
                x if span == 1 else x.reshape(outer, span, block, col_width)[:, n].reshape(
                    outer * block, col_width
                )
                for x in (same, other)
            ]
            operands = [place, *pair_rows, gain, gate_weight[0], up_weight[0], *carry]
            carry = pl.pallas_call(
                functools.partial(multiply_kernel, plan),
                out_shape=(
                    [jax.ShapeDtypeStruct((rows_all, ffe), jnp.bfloat16)]
                    if last
                    else [sum_shape, sum_shape, square_shape]
                ),
                in_specs=[scalars] + [whole] * (len(operands) - 1),
                out_specs=[whole] * (1 if last else 3),
                scratch_shapes=[
                    pltpu.VMEM((rows_all, col_width), jnp.bfloat16),
                    pltpu.VMEM((rows_all, 128), jnp.float32),
                ],
                compiler_params=pltpu.CompilerParams(vmem_limit_bytes=24 * 1024 * 1024),
                name="multiply",
            )(*operands)
    active = carry[0].reshape(exp_count, req_count, own_rows, ffe)

    own = [piece[:own_rows] for piece in pieces]
    if aligned:
        own = [p[b * own_rows : (b + 1) * own_rows] for b, p in enumerate(pieces)]
    own = jnp.stack(own)[req_rel]
    total = own.transpose(1, 0, 2).reshape(own_rows, width).astype(jnp.float32)
    previous = extra
    for j in reversed(range(0, req_count, span)):
        rows = active[:, j : j + span].reshape(span * tok_rows, ffe)
        row_weight = weight_all[:, j : j + span].reshape(span * tok_rows, 1)
        cut = span * tok_rows // 2
        give, keep = pl.pallas_call(
            down_kernel,
            out_shape=[
                jax.ShapeDtypeStruct((cut, width), jnp.bfloat16),
                jax.ShapeDtypeStruct((cut, width), jnp.float32),
            ],
            in_specs=[whole, whole, whole, somewhere],
            out_specs=[whole, whole],
            compiler_params=pltpu.CompilerParams(vmem_limit_bytes=24 * 1024 * 1024),
            name="down",
        )(rows, down_weight[0], row_weight, previous)
        previous = give
        pair_sum = keep + swap(give, "exp", 1).astype(jnp.float32)
        sums = scatter_outer(pair_sum.reshape(outer, span * own_rows, width))
        for n in reversed(range(span)):
            part = sums[n * own_rows : (n + 1) * own_rows]
            if j + n:
                part = swap(part.astype(jnp.bfloat16), "req", j + n).astype(jnp.float32)
            total = total + part
    return total.astype(jnp.bfloat16)


def solution(mesh):
    return jax.shard_map(
        local,
        mesh=mesh,
        in_specs=(
            P("req", "exp"),
            P("req", None),
            P("req", None),
            P(),
            P(),
            P(("req", "exp"), None),
            P(),
            P("exp", None, None),
            P("exp", "req"),
            P("req", None),
            P("req", None),
            P("exp", None, "req"),
            P("exp", None, "req"),
            P("exp", "req", None),
        ),
        out_specs=P(("req", "exp"), None),
        check_vma=False,
    )
```

```python
import functools

import jax
import jax.numpy as jnp
import numpy as np
from jax import lax
from jax.experimental import pallas as pl
from jax.experimental.pallas import tpu as pltpu
from jax.sharding import PartitionSpec as P

score_scale = 192.0 ** (-0.5)
norm_eps = 1e-06


def swap(x, axis, distance):
    size = lax.axis_size(axis)
    return lax.ppermute(x, axis, [(i, i ^ distance) for i in range(size)])


def pick_kernel(plan, place, lists, pool, *outs):
    req_count, per_index, depth_here, pool_rows, width, far_width, far_split, near_split = plan
    slots = per_index * depth_here
    req_index = place[0]
    row = lax.broadcasted_iota(jnp.int32, (16, pool_rows), 0)
    column = lax.broadcasted_iota(jnp.int32, (16, pool_rows), 1)

    def wanted(target):
        hot = row < 0
        for slot in range(slots):
            request, depth = slot // depth_here, slot % depth_here
            page = lists[target * per_index + request, req_index * depth_here + depth]
            hot = hot | ((row == slot) & (column == page - req_index * pool_rows))
        return hot.astype(jnp.float32)

    piece = far_width // far_split
    for out, j in zip(outs, range(1, req_count)):
        hot = wanted(req_index ^ j)
        total = jnp.zeros((16, piece), jnp.float32)
        for part in range(far_split):
            shifted = hot if part == 0 else pltpu.roll(hot, part * slots, 0)
            total = total + jnp.dot(
                shifted.astype(jnp.bfloat16),
                pool[:, part * piece : (part + 1) * piece],
                preferred_element_type=jnp.float32,
            )
        out[...] = total.astype(jnp.bfloat16)


def near_kernel(plan, place, lists, pool, out):
    req_count, per_index, depth_here, pool_rows, width, far_width, far_split, near_split = plan
    slots = per_index * depth_here
    req_index = place[0]
    row = lax.broadcasted_iota(jnp.int32, (16, pool_rows), 0)
    column = lax.broadcasted_iota(jnp.int32, (16, pool_rows), 1)
    hots = [row < 0] * near_split
    for slot in range(slots):
        request, depth = slot // depth_here, slot % depth_here
        page = lists[req_index * per_index + request, req_index * depth_here + depth]
        here = column == page - req_index * pool_rows
        for part in range(near_split):
            hots[part] = hots[part] | ((row == part * slots + slot) & here)
    hots = [hot.astype(jnp.float32).astype(jnp.bfloat16) for hot in hots]
    piece = width // near_split
    step = 1152
    for start in range(0, piece, step):
        total = jnp.zeros((16, step), jnp.float32)
        for part in range(near_split):
            cols = slice(part * piece + start, part * piece + start + step)
            total = total + jnp.dot(hots[part], pool[:, cols], preferred_element_type=jnp.float32)
        out[:, start : start + step] = total.astype(jnp.bfloat16)


def attention_kernel(
    plan, place, near, far, new, q_even, q_odd, bias_even, bias_odd, bias_new, uv, extra, out,
    k_even, k_odd, s_even, s_odd, heads,
):
    per_index, latent, kv_rank, head_here, tok_rows, order, own_rows = plan
    pair = 2 * latent
    window = latent + 64
    lead = pair - window
    units, far_rows, far_width = far.shape
    near_rows = near.shape[0]
    base = 0

    def place_keys(rows, value_of, pairs, base):
        for p in range(pairs):
            k_even[base : base + rows, :] = value_of(p * pair, p * pair + window)
            k_odd[base : base + rows, :] = value_of(p * pair + lead, (p + 1) * pair)
            base += rows
        return base

    base = place_keys(near_rows, lambda a, b: near[:, a:b], near.shape[1] // pair, base)
    for m in range(units):
        base = place_keys(far_rows, lambda a, b: far[m, :, a:b], far_width // pair, base)
    rows_k = (((1,), (1,)), ((), ()))

    def times(a, b):
        return lax.dot_general(a, b, rows_k, preferred_element_type=jnp.float32) * score_scale

    s_even[...] = times(q_even[...], k_even[...])
    s_odd[...] = times(q_odd[...], k_odd[...])
    s_new = times(q_even[...], new[...])
    new_count = tok_rows // per_index
    p_even, p_odd, p_new = [], [], []
    for h in range(head_here):
        for i in range(per_index):
            at = h * tok_rows + i * new_count
            rows = slice(at, at + new_count)
            even = s_even[rows, :] + bias_even[i : i + 1, :]
            odd = s_odd[rows, :] + bias_odd[i : i + 1, :]
            fresh = s_new[rows, :] + bias_new[i * new_count : (i + 1) * new_count, :]
            top = jnp.maximum(
                jnp.max(jnp.maximum(even, odd), axis=-1, keepdims=True),
                jnp.max(fresh, axis=-1, keepdims=True),
            )
            even, odd, fresh = jnp.exp(even - top), jnp.exp(odd - top), jnp.exp(fresh - top)
            share = 1.0 / (
                jnp.sum(even + odd, axis=-1, keepdims=True)
                + jnp.sum(fresh, axis=-1, keepdims=True)
            )
            p_even.append((even * share).astype(jnp.bfloat16))
            p_odd.append((odd * share).astype(jnp.bfloat16))
            p_new.append((fresh * share).astype(jnp.bfloat16))
    p_even, p_odd, p_new = (jnp.concatenate(p, axis=0) for p in (p_even, p_odd, p_new))
    first = jnp.dot(p_even, k_even[:, :kv_rank], preferred_element_type=jnp.float32)
    second = jnp.dot(p_odd, k_odd[...], preferred_element_type=jnp.float32)
    third = jnp.dot(p_new, new[:, :kv_rank], preferred_element_type=jnp.float32)
    latent_out = (first + third + second[:, 64 : 64 + kv_rank]).astype(jnp.bfloat16)
    value_width = uv.shape[2]
    for h in range(head_here):
        heads[:, h * value_width : (h + 1) * value_width] = jnp.dot(
            latent_out[h * tok_rows : (h + 1) * tok_rows],
            uv[h],
            preferred_element_type=jnp.float32,
        )
    out[tok_rows:, :] = extra[...]
    if own_rows % 8:
        out[:tok_rows, :] = heads[...].astype(jnp.bfloat16)
        return
    exp_index = place[1]
    blocks = []
    for m in order:
        at = (exp_index ^ m) * own_rows
        blocks.append(heads[pl.ds(pl.multiple_of(at, 8), own_rows), :])
    out[:tok_rows, :] = jnp.concatenate(blocks, axis=0).astype(jnp.bfloat16)


def hold_kernel(x, other, out):
    del other
    out[...] = x[...]


def collect_kernel(count, *refs):
    out, base = refs[-1], 0
    for ref in refs[:count]:
        out[base : base + ref.shape[0], :] = ref[...]
        base += ref.shape[0]


def project_kernel(plan, *refs):
    req_count, exp_count, own_rows = plan
    heads, (weight, keep, give, rows, held, sem) = refs[:req_count], refs[req_count:]
    fetch = pltpu.make_async_copy(weight, held, sem)
    fetch.start()
    for j in range(req_count):
        for m in range(exp_count):
            at = (m * req_count + j) * own_rows
            rows[at : at + own_rows, :] = heads[j][m * own_rows : (m + 1) * own_rows, :]
    fetch.wait()
    half = keep.shape[0]
    for n in range(0, keep.shape[1], 256):
        cols = slice(n, n + 256)
        out = jnp.dot(rows[...], held[:, cols], preferred_element_type=jnp.float32)
        keep[:, cols] = out[:half]
        give[:, cols] = out[half:].astype(jnp.bfloat16)


def pair_kernel(keep, got, *outs):
    rows = outs[0].shape[0]
    for k, out in enumerate(outs):
        at = slice(k * rows, (k + 1) * rows)
        out[...] = (keep[at, :] + got[at, :].astype(jnp.float32)).astype(out.dtype)


def hidden_kernel(req_count, place, hidden, other, *outs):
    del other
    columns = outs[0].shape[1]
    for j in range(req_count):
        start = pl.multiple_of((place[0] ^ j) * columns, 128)
        outs[j][...] = hidden[:, pl.ds(start, columns)]


def resid_kernel(own, *refs):
    req_count = 4
    sums, hidden, outs = refs[:3], refs[3 : 3 + req_count], refs[3 + req_count :]
    rows = hidden[0].shape[0]
    in_chunk = req_count // len(outs)
    for j in range(req_count):
        at = slice(j * rows, (j + 1) * rows)
        total = own[at, :]
        for ref in sums:
            total = total + ref[at, :].astype(jnp.float32)
        total = (hidden[j][...].astype(jnp.float32) + total).astype(jnp.bfloat16)
        to = j % in_chunk * rows
        outs[j // in_chunk][to : to + rows, :] = total


def norm_kernel(plan, place, gain, *refs):
    req_count, own_rows, others = plan
    pieces, (left, right, first, full) = refs[:req_count], refs[req_count + others :]
    rows, columns = pieces[0].shape
    in_chunk = rows // own_rows
    width = columns * req_count
    for b, piece in enumerate(pieces):
        start = pl.multiple_of((place[0] ^ b) * columns, 128)
        for n in range(in_chunk):
            m = n ^ (b % in_chunk)
            got = piece[m * own_rows : (m + 1) * own_rows, :]
            full[n * own_rows : (n + 1) * own_rows, pl.ds(start, columns)] = got
    first[...] = full[:own_rows, :]
    half = width // 2
    for n in range(in_chunk):
        at = slice(n * own_rows, (n + 1) * own_rows)
        widened = full[at, :].astype(jnp.float32)
        mean = jnp.sum(widened * widened, axis=-1, keepdims=True) / width
        normed = (widened * lax.rsqrt(mean + norm_eps) * gain[...]).astype(jnp.bfloat16)
        left[at, :] = normed[:, :half]
        right[at, :] = normed[:, half:]


def local(
    queries,
    new_latent,
    pool,
    page_list,
    prefix_len,
    hidden_in,
    norm_gain,
    uv_weight,
    out_weight,
    route_ids,
    route_weight,
    gate_weight,
    up_weight,
    down_weight,
):
    req_count = lax.axis_size("req")
    exp_count = lax.axis_size("exp")
    req_index = lax.axis_index("req")
    exp_index = lax.axis_index("exp")
    tok_rows = queries.shape[0]
    latent = new_latent.shape[1]
    kv_rank = uv_weight.shape[1]
    value_width = uv_weight.shape[2]
    head_here = uv_weight.shape[0]
    pool_rows = pool.shape[0]
    page_size = pool.shape[1] // latent
    list_depth = page_list.shape[1]
    per_index = page_list.shape[0] // req_count
    depth_here = list_depth // req_count
    width = hidden_in.shape[1]
    col_width = width // req_count
    half_width = width // 2
    own_rows = tok_rows // exp_count
    outer = exp_count // 2
    req_rel = req_index ^ jnp.arange(req_count, dtype=jnp.int32)
    rel_order = [2 * k for k in range(outer)] + [2 * k + 1 for k in range(outer)]
    exp_rel = exp_index ^ jnp.array(rel_order, dtype=jnp.int32)

    slots = per_index * depth_here
    pair = 2 * latent
    pool_width = pool.shape[1]
    far_width = pool_width // exp_count
    far_split = min(16 // slots, far_width // pair)
    near_split = 16 // slots
    lengths = prefix_len.reshape(req_count, per_index)
    place = jnp.stack([req_index, exp_index]).astype(jnp.int32)
    plan = (
        req_count, per_index, depth_here, pool_rows, pool_width, far_width, far_split, near_split,
    )
    scalars = pl.BlockSpec(memory_space=pltpu.SMEM)
    whole = pl.BlockSpec(memory_space=pltpu.VMEM)
    far_shape = jax.ShapeDtypeStruct((16, far_width // far_split), jnp.bfloat16)
    sent = pl.pallas_call(
        functools.partial(pick_kernel, plan),
        out_shape=[far_shape] * (req_count - 1),
        grid_spec=pltpu.PrefetchScalarGridSpec(
            num_scalar_prefetch=2,
            grid=(1,),
            in_specs=[pl.BlockSpec((pool_rows, far_width), lambda n, place, lists: (0, place[1]))],
            out_specs=[whole] * (req_count - 1),
        ),
        name="pick_far",
    )(place, page_list, pool)
    near = pl.pallas_call(
        functools.partial(near_kernel, plan),
        out_shape=jax.ShapeDtypeStruct((16, pool_width // near_split), jnp.bfloat16),
        in_specs=[scalars, scalars, whole],
        out_specs=whole,
        name="pick_near",
    )(place, page_list, pool)
    far = jnp.concatenate([swap(sent[j - 1], "req", j) for j in range(1, req_count)], axis=0)
    far_out = jnp.stack([far] + [swap(far, "exp", 2 * k) for k in range(1, outer)])
    far_all = jnp.concatenate([far_out, swap(far_out, "exp", 1)], axis=0)

    def positions(tokens, holder_ids, split, slot_row):
        depth = holder_ids * depth_here + slot_row % slots % depth_here
        return jnp.where(slot_row < slots * split, depth * page_size + tokens, list_depth * page_size)

    chosen = route_ids == exp_index
    token_weight = jnp.sum(jnp.where(chosen, route_weight, 0.0), axis=1)
    token_weight = token_weight.reshape(exp_count, own_rows)[exp_rel].reshape(-1)
    parts, left = [], token_weight
    for n in range(3):
        part = lax.reduce_precision(left, 8, 7)
        left = left - part
        parts.append(part.astype(jnp.bfloat16))
    head_cols = head_here * value_width
    extra_rows = -(-3 * tok_rows // (16 * head_cols)) * 16
    extra = jnp.concatenate(parts)
    extra = jnp.pad(extra, (0, extra_rows * head_cols - 3 * tok_rows))
    extra = extra.reshape(extra_rows, head_cols)

    near_piece = page_size // near_split
    pairs = np.arange(near_piece // 2)[:, None]
    slot_row = np.arange(16)[None, :]
    near_pos = positions(slot_row // slots * near_piece + 2 * pairs, req_index, near_split, slot_row)
    near_req = np.broadcast_to(slot_row % slots // depth_here, near_pos.shape)
    far_tokens = page_size // exp_count
    far_piece = far_tokens // far_split
    pairs = np.arange(far_piece // 2).reshape(1, -1, 1, 1)
    slot_row = np.arange(16).reshape(1, 1, 1, -1)
    far_pos = positions(
        exp_rel.reshape(-1, 1, 1, 1) * far_tokens + slot_row // slots * far_piece + 2 * pairs,
        req_rel[1:].reshape(1, 1, -1, 1),
        far_split,
        slot_row,
    )
    far_req = np.broadcast_to(slot_row % slots // depth_here, far_pos.shape)
    key_pos = jnp.concatenate([near_pos.reshape(1, -1), far_pos.reshape(1, -1)], axis=1)
    key_req = np.concatenate([near_req.reshape(1, -1), far_req.reshape(1, -1)], axis=1)
    my_lengths = lax.dynamic_index_in_dim(lengths, req_index, 0, keepdims=False)[:, None]
    same = key_req == np.arange(per_index)[:, None]
    bias_even = jnp.where(same & (key_pos < my_lengths), 0.0, -1e30)
    bias_odd = jnp.where(same & (key_pos + 1 < my_lengths), 0.0, -1e30)
    new_count = tok_rows // per_index
    tok = np.arange(tok_rows)
    seen = (tok[:, None] // new_count == tok // new_count) & (tok <= tok[:, None])
    bias_new = jnp.asarray(np.where(seen, 0.0, -1e30), jnp.float32)
    by_head = queries.reshape(tok_rows, head_here, latent).transpose(1, 0, 2)
    by_head = by_head.reshape(head_here * tok_rows, latent)
    q_even = jnp.pad(by_head, ((0, 0), (0, 64)))
    q_odd = jnp.pad(by_head, ((0, 0), (64, 0)))
    new_keys = jnp.pad(new_latent, ((0, 0), (0, 64)))
    key_count = key_req.shape[1]
    q_rows = head_here * tok_rows
    head_out = pl.pallas_call(
        functools.partial(
            attention_kernel,
            (
                per_index, latent, kv_rank, head_here, tok_rows, tuple(rel_order), own_rows,
            ),
        ),
        out_shape=jax.ShapeDtypeStruct((tok_rows + extra_rows, head_cols), jnp.bfloat16),
        in_specs=[scalars] + [whole] * 10,
        out_specs=whole,
        scratch_shapes=[
            pltpu.VMEM((key_count, latent + 64), jnp.bfloat16),
            pltpu.VMEM((key_count, latent + 64), jnp.bfloat16),
            pltpu.VMEM((q_rows, key_count), jnp.float32),
            pltpu.VMEM((q_rows, key_count), jnp.float32),
            pltpu.VMEM((tok_rows, head_cols), jnp.float32),
        ],
        compiler_params=pltpu.CompilerParams(vmem_limit_bytes=12 * 1024 * 1024),
        name="attention",
    )(place, near, far_all, new_keys, q_even, q_odd, bias_even, bias_odd, bias_new, uv_weight, extra)
    if own_rows % 8:
        ordered = head_out[:tok_rows].reshape(exp_count, own_rows, head_cols)[exp_rel]
        head_out = jnp.concatenate([ordered.reshape(tok_rows, head_cols), head_out[tok_rows:]])

    heads = [head_out] + [swap(head_out, "req", j) for j in range(1, req_count)]
    weight_all = jnp.stack([h[tok_rows:].reshape(-1)[: 3 * tok_rows] for h in heads])
    weight_all = weight_all.astype(jnp.float32).reshape(req_count, 3, exp_count, own_rows)
    weight_all = (weight_all[:, 0] + weight_all[:, 1] + weight_all[:, 2]).transpose(1, 0, 2)
    block = req_count * own_rows
    aligned = own_rows % 16 == 0 and outer == 4
    somewhere = pl.BlockSpec(memory_space=pl.ANY)
    in_hbm = pl.BlockSpec(memory_space=pltpu.HBM)
    cut = outer * block

    def grant(mib):
        return pltpu.CompilerParams(vmem_limit_bytes=mib * 1024 * 1024)

    def pair_blocks(keep, got):
        rows, columns = keep.shape[0] // 4, keep.shape[1]
        return pl.pallas_call(
            pair_kernel,
            out_shape=[jax.ShapeDtypeStruct((rows, columns), jnp.float32)]
            + [jax.ShapeDtypeStruct((rows, columns), jnp.bfloat16)] * 3,
            in_specs=[whole, whole],
            out_specs=[whole] * 4,
            compiler_params=grant(4),
            name="pair",
        )(keep, got)

    if aligned:
        keep, give = pl.pallas_call(
            functools.partial(project_kernel, (req_count, exp_count, own_rows)),
            out_shape=[
                jax.ShapeDtypeStruct((cut, col_width), jnp.float32),
                jax.ShapeDtypeStruct((cut, col_width), jnp.bfloat16),
            ],
            in_specs=[whole] * req_count + [in_hbm],
            out_specs=[whole, whole],
            scratch_shapes=[
                pltpu.VMEM((2 * cut, head_cols), jnp.bfloat16),
                pltpu.VMEM(out_weight.shape, jnp.bfloat16),
                pltpu.SemaphoreType.DMA,
            ],
            compiler_params=grant(6),
            name="project",
        )(*heads, out_weight)
        parts = pair_blocks(keep, swap(give, "exp", 1))
    else:
        heads_all = jnp.stack(
            [h[:tok_rows].reshape(exp_count, own_rows, head_cols) for h in heads], axis=1
        )
        partial = jnp.dot(
            heads_all.reshape(exp_count * block, head_cols),
            out_weight,
            preferred_element_type=jnp.float32,
        )
        other = swap(partial[cut:].astype(jnp.bfloat16), "exp", 1)
        parts = partial[:cut] + other.astype(jnp.float32)
        parts = list(parts.reshape(outer, block, col_width))
    chunks = 2
    in_chunk = req_count // chunks
    chunk_block = in_chunk * own_rows
    along = [swap(parts[k].astype(jnp.bfloat16), "exp", 2 * k) for k in range(1, outer)]

    def collect(blocks, others):
        rows = sum(x.shape[0] for x in blocks)
        return pl.pallas_call(
            functools.partial(collect_kernel, len(blocks)),
            out_shape=jax.ShapeDtypeStruct((rows, blocks[0].shape[1]), blocks[0].dtype),
            in_specs=[whole] * len(blocks) + [somewhere] * len(others),
            out_specs=whole,
            compiler_params=grant(2),
            name="collect",
        )(*blocks, *others)

    if aligned and in_chunk == 2:
        hidden = pl.pallas_call(
            functools.partial(hidden_kernel, req_count),
            out_shape=[jax.ShapeDtypeStruct((own_rows, col_width), jnp.bfloat16)] * req_count,
            in_specs=[scalars, whole, somewhere],
            out_specs=[whole] * req_count,
            compiler_params=grant(2),
            name="hidden",
        )(place, hidden_in, parts[0])
        hidden = [x if j == 0 else swap(x, "req", j) for j, x in enumerate(hidden)]
        resid = pl.pallas_call(
            resid_kernel,
            out_shape=[jax.ShapeDtypeStruct((chunk_block, col_width), jnp.bfloat16)] * chunks,
            in_specs=[whole] * (4 + req_count),
            out_specs=[whole] * chunks,
            compiler_params=grant(2),
            name="resid",
        )(parts[0], *along, *hidden)
        gain = norm_gain.astype(jnp.float32).reshape(1, width)

        def normalise(c, after_slices, after_norm):
            sent = resid
            if after_slices:
                sent = [collect([x], after_slices) for x in resid]
            slices = [resid[c]]
            for b in range(1, req_count):
                slices.append(swap(sent[c ^ b // in_chunk], "req", b))
            half_shape = jax.ShapeDtypeStruct((chunk_block, half_width), jnp.bfloat16)
            *halves, first = pl.pallas_call(
                functools.partial(norm_kernel, (req_count, own_rows, len(after_norm))),
                out_shape=[half_shape, half_shape]
                + [jax.ShapeDtypeStruct((own_rows, width), jnp.bfloat16)],
                in_specs=[scalars] + [whole] * (1 + req_count) + [somewhere] * len(after_norm),
                out_specs=[whole] * 3,
                scratch_shapes=[pltpu.VMEM((chunk_block, width), jnp.bfloat16)],
                compiler_params=grant(4),
                name="norm",
            )(place, gain, *slices, *after_norm)
            return slices, halves, first
    else:
        hidden = [
            lax.dynamic_slice_in_dim(hidden_in, req_rel[j] * col_width, col_width, 1)
            for j in range(req_count)
        ]
        hidden = [x if j == 0 else swap(x, "req", j) for j, x in enumerate(hidden)]
        attn = sum([x.astype(jnp.float32) for x in along], parts[0])
        resid = jnp.concatenate(hidden, axis=0).astype(jnp.float32) + attn
        resid = resid.astype(jnp.bfloat16)
        pieces = [resid]
        for b in range(1, req_count):
            got = swap(resid, "req", b).reshape(req_count, own_rows, col_width)
            pieces.append(jnp.concatenate([got[i ^ b] for i in range(req_count)], axis=0))
        full = jnp.stack(pieces)[req_rel].transpose(1, 0, 2).reshape(block, width)
        widened = full.astype(jnp.float32)
        inv_scale = lax.rsqrt(jnp.mean(widened * widened, axis=-1, keepdims=True) + norm_eps)
        normed = (widened * inv_scale * norm_gain.astype(jnp.float32)).astype(jnp.bfloat16)
        normed = normed.reshape(chunks, chunk_block, 2, half_width)

        def normalise(c, after_slices, after_norm):
            return [], [normed[c, :, n] for n in range(2)], full[:own_rows]

    outer_bits = []
    bit = 1
    while bit < outer:
        outer_bits.append(bit)
        bit *= 2
    orders = (outer_bits, outer_bits[::-1])

    def gather_plane(piece, bits, others):
        held = piece[None]
        ids = [0]
        firsts = []
        for bit in bits:
            firsts.append(swap(held, "exp", 2 * bit))
            held = jnp.concatenate([held, firsts[-1]], axis=0)
            ids = ids + [k ^ bit for k in ids]
        same = [held[ids.index(k)] for k in range(outer)]
        same = collect(same, others) if others else jnp.concatenate(same, axis=0)
        return jnp.concatenate([same, swap(same, "exp", 1)], axis=0), firsts[0]

    def scatter_plane(partial, bits):
        cut = outer * chunk_block
        other = swap(partial[cut:].astype(jnp.bfloat16), "exp", 1)
        held = (partial[:cut] + other.astype(jnp.float32)).reshape(outer, chunk_block, half_width)
        ids = list(range(outer))
        firsts = []
        for bit in bits:
            keep = [n for n, k in enumerate(ids) if not k & bit]
            give = [ids.index(ids[n] ^ bit) for n in keep]
            sent = swap(jnp.stack([held[n] for n in give]).astype(jnp.bfloat16), "exp", 2 * bit)
            firsts.append(sent)
            held = jnp.stack([held[n] for n in keep]) + sent.astype(jnp.float32)
            ids = [ids[n] for n in keep]
        return held[0].astype(jnp.bfloat16), firsts[0]

    gate_here = gate_weight[0]
    up_here = up_weight[0]
    down_here = down_weight[0]
    total = 0.0
    slices, arrived, before_gather, before_down = [], [], [], []
    for c in reversed(range(chunks)):
        slices, halves, resid_own = normalise(c, slices[1:], arrived)
        (left, *arrived), (right, *last) = (
            gather_plane(halves[n], orders[n], before_gather) for n in range(2)
        )
        arrived = arrived + last

        def project(matrix):
            return jnp.dot(
                left, matrix[:half_width], preferred_element_type=jnp.float32
            ) + jnp.dot(right, matrix[half_width:], preferred_element_type=jnp.float32)

        active = (jax.nn.silu(project(gate_here)) * project(up_here)).astype(jnp.bfloat16)
        if before_down:
            active = collect([active], before_down)
        reqs = range(c * in_chunk, (c + 1) * in_chunk)
        row_weight = weight_all[:, reqs[0] : reqs[-1] + 1].reshape(-1, 1)
        sides, before_gather, before_down = [], [], []
        for n in range(2):
            cols = slice(n * half_width, (n + 1) * half_width)
            out = jnp.dot(active, down_here[:, cols], preferred_element_type=jnp.float32)
            out = out * row_weight
            before_gather.append(out)
            side, first = scatter_plane(out, orders[n])
            sides.append(side)
            before_down.append(first)
        sums = jnp.concatenate(sides, axis=1)
        for n, j in reversed(list(enumerate(reqs))):
            part = sums[n * own_rows : (n + 1) * own_rows]
            if j:
                part = swap(part, "req", j)
            total = total + part.astype(jnp.float32)
    return (total + resid_own.astype(jnp.float32)).astype(jnp.bfloat16)


def solution(mesh):
    return jax.shard_map(
        local,
        mesh=mesh,
        in_specs=(
            P("req", "exp"),
            P("req", None),
            P("req", None),
            P(),
            P(),
            P(("req", "exp"), None),
            P(),
            P("exp", None, None),
            P("exp", "req"),
            P("req", None),
            P("req", None),
            P("exp", None, "req"),
            P("exp", None, "req"),
            P("exp", "req", None),
        ),
        out_specs=P(("req", "exp"), None),
        check_vma=False,
    )
```

```python
import functools

import jax
import jax.numpy as jnp
import numpy as np
from jax import lax
from jax.experimental import pallas as pl
from jax.experimental.pallas import tpu as pltpu
from jax.sharding import PartitionSpec as P

score_scale = 192.0 ** (-0.5)
norm_eps = 1e-06


def swap(x, axis, distance):
    size = lax.axis_size(axis)
    return lax.ppermute(x, axis, [(i, i ^ distance) for i in range(size)])


def pick_kernel(plan, place, lists, pool, *outs):
    req_count, per_index, depth_here, pool_rows, width, far_width, far_split, near_split = plan
    slots = per_index * depth_here
    req_index = place[0]
    row = lax.broadcasted_iota(jnp.int32, (16, pool_rows), 0)
    column = lax.broadcasted_iota(jnp.int32, (16, pool_rows), 1)

    def wanted(target):
        hot = row < 0
        for slot in range(slots):
            request, depth = slot // depth_here, slot % depth_here
            page = lists[target * per_index + request, req_index * depth_here + depth]
            hot = hot | ((row == slot) & (column == page - req_index * pool_rows))
        return hot.astype(jnp.float32)

    piece = far_width // far_split
    for out, j in zip(outs, range(1, req_count)):
        hot = wanted(req_index ^ j)
        total = jnp.zeros((16, piece), jnp.float32)
        for part in range(far_split):
            shifted = hot if part == 0 else pltpu.roll(hot, part * slots, 0)
            total = total + jnp.dot(
                shifted.astype(jnp.bfloat16),
                pool[:, part * piece : (part + 1) * piece],
                preferred_element_type=jnp.float32,
            )
        out[...] = total.astype(jnp.bfloat16)


def near_kernel(plan, place, lists, pool, out):
    req_count, per_index, depth_here, pool_rows, width, far_width, far_split, near_split = plan
    slots = per_index * depth_here
    req_index = place[0]
    row = lax.broadcasted_iota(jnp.int32, (16, pool_rows), 0)
    column = lax.broadcasted_iota(jnp.int32, (16, pool_rows), 1)
    hots = [row < 0] * near_split
    for slot in range(slots):
        request, depth = slot // depth_here, slot % depth_here
        page = lists[req_index * per_index + request, req_index * depth_here + depth]
        here = column == page - req_index * pool_rows
        for part in range(near_split):
            hots[part] = hots[part] | ((row == part * slots + slot) & here)
    hots = [hot.astype(jnp.float32).astype(jnp.bfloat16) for hot in hots]
    piece = width // near_split
    step = 1152
    for start in range(0, piece, step):
        total = jnp.zeros((16, step), jnp.float32)
        for part in range(near_split):
            cols = slice(part * piece + start, part * piece + start + step)
            total = total + jnp.dot(hots[part], pool[:, cols], preferred_element_type=jnp.float32)
        out[:, start : start + step] = total.astype(jnp.bfloat16)


def attention_kernel(
    plan, place, near, far, new, q_even, q_odd, bias_even, bias_odd, bias_new, uv, extra, out,
    k_even, k_odd, s_even, s_odd, heads,
):
    per_index, latent, kv_rank, head_here, tok_rows, order, own_rows = plan
    pair = 2 * latent
    window = latent + 64
    lead = pair - window
    units, far_rows, far_width = far.shape
    near_rows = near.shape[0]
    base = 0

    def place_keys(rows, value_of, pairs, base):
        for p in range(pairs):
            k_even[base : base + rows, :] = value_of(p * pair, p * pair + window)
            k_odd[base : base + rows, :] = value_of(p * pair + lead, (p + 1) * pair)
            base += rows
        return base

    base = place_keys(near_rows, lambda a, b: near[:, a:b], near.shape[1] // pair, base)
    for m in range(units):
        base = place_keys(far_rows, lambda a, b: far[m, :, a:b], far_width // pair, base)
    rows_k = (((1,), (1,)), ((), ()))

    def times(a, b):
        return lax.dot_general(a, b, rows_k, preferred_element_type=jnp.float32) * score_scale

    s_even[...] = times(q_even[...], k_even[...])
    s_odd[...] = times(q_odd[...], k_odd[...])
    s_new = times(q_even[...], new[...])
    new_count = tok_rows // per_index
    p_even, p_odd, p_new = [], [], []
    for h in range(head_here):
        for i in range(per_index):
            at = h * tok_rows + i * new_count
            rows = slice(at, at + new_count)
            even = s_even[rows, :] + bias_even[i : i + 1, :]
            odd = s_odd[rows, :] + bias_odd[i : i + 1, :]
            fresh = s_new[rows, :] + bias_new[i * new_count : (i + 1) * new_count, :]
            top = jnp.maximum(
                jnp.max(jnp.maximum(even, odd), axis=-1, keepdims=True),
                jnp.max(fresh, axis=-1, keepdims=True),
            )
            even, odd, fresh = jnp.exp(even - top), jnp.exp(odd - top), jnp.exp(fresh - top)
            share = 1.0 / (
                jnp.sum(even + odd, axis=-1, keepdims=True)
                + jnp.sum(fresh, axis=-1, keepdims=True)
            )
            p_even.append((even * share).astype(jnp.bfloat16))
            p_odd.append((odd * share).astype(jnp.bfloat16))
            p_new.append((fresh * share).astype(jnp.bfloat16))
    p_even, p_odd, p_new = (jnp.concatenate(p, axis=0) for p in (p_even, p_odd, p_new))
    first = jnp.dot(p_even, k_even[:, :kv_rank], preferred_element_type=jnp.float32)
    second = jnp.dot(p_odd, k_odd[...], preferred_element_type=jnp.float32)
    third = jnp.dot(p_new, new[:, :kv_rank], preferred_element_type=jnp.float32)
    latent_out = (first + third + second[:, 64 : 64 + kv_rank]).astype(jnp.bfloat16)
    value_width = uv.shape[2]
    for h in range(head_here):
        heads[:, h * value_width : (h + 1) * value_width] = jnp.dot(
            latent_out[h * tok_rows : (h + 1) * tok_rows],
            uv[h],
            preferred_element_type=jnp.float32,
        )
    out[tok_rows:, :] = extra[...]
    if own_rows % 8:
        out[:tok_rows, :] = heads[...].astype(jnp.bfloat16)
        return
    exp_index = place[1]
    blocks = []
    for m in order:
        at = (exp_index ^ m) * own_rows
        blocks.append(heads[pl.ds(pl.multiple_of(at, 8), own_rows), :])
    out[:tok_rows, :] = jnp.concatenate(blocks, axis=0).astype(jnp.bfloat16)


def hold_kernel(x, other, out):
    del other
    out[...] = x[...]


def collect_kernel(count, *refs):
    out, base = refs[-1], 0
    for ref in refs[:count]:
        out[base : base + ref.shape[0], :] = ref[...]
        base += ref.shape[0]


def pick_blocks_kernel(picks, count, *refs):
    out, base = refs[-1], 0
    for k, n in picks:
        rows = refs[k].shape[-2]
        out[base : base + rows, :] = refs[k][n]
        base += rows


def project_kernel(plan, *refs):
    req_count, exp_count, own_rows = plan
    heads, (weight, keep, give, rows, held, sem) = refs[:req_count], refs[req_count:]
    fetch = pltpu.make_async_copy(weight, held, sem)
    fetch.start()
    for j in range(req_count):
        for m in range(exp_count):
            at = (m * req_count + j) * own_rows
            rows[at : at + own_rows, :] = heads[j][m * own_rows : (m + 1) * own_rows, :]
    fetch.wait()
    half = keep.shape[0]
    for n in range(0, keep.shape[1], 256):
        cols = slice(n, n + 256)
        out = jnp.dot(rows[...], held[:, cols], preferred_element_type=jnp.float32)
        keep[:, cols] = out[:half]
        give[:, cols] = out[half:].astype(jnp.bfloat16)


def pair_kernel(place, keep, got, hidden, *outs):
    rows = outs[0].shape[0]
    for k, out in enumerate(outs[:4]):
        at = slice(k * rows, (k + 1) * rows)
        out[...] = (keep[at, :] + got[at, :].astype(jnp.float32)).astype(out.dtype)
    columns = outs[0].shape[1]
    for j, out in enumerate(outs[4:]):
        start = pl.multiple_of((place[0] ^ j) * columns, 128)
        out[...] = hidden[:, pl.ds(start, columns)]


def resid_kernel(own, *refs):
    req_count = 4
    sums, hidden, outs = refs[:3], refs[3 : 3 + req_count], refs[3 + req_count :]
    rows = hidden[0].shape[0]
    in_chunk = req_count // len(outs)
    for j in range(req_count):
        at = slice(j * rows, (j + 1) * rows)
        total = own[at, :]
        for ref in sums:
            total = total + ref[at, :].astype(jnp.float32)
        total = (hidden[j][...].astype(jnp.float32) + total).astype(jnp.bfloat16)
        to = j % in_chunk * rows
        outs[j // in_chunk][to : to + rows, :] = total


def norm_kernel(plan, place, gain, *refs):
    req_count, own_rows, others = plan
    pieces, (left, right, first, full) = refs[:req_count], refs[req_count + others :]
    rows, columns = pieces[0].shape
    in_chunk = rows // own_rows
    width = columns * req_count
    for b, piece in enumerate(pieces):
        start = pl.multiple_of((place[0] ^ b) * columns, 128)
        for n in range(in_chunk):
            m = n ^ (b % in_chunk)
            got = piece[m * own_rows : (m + 1) * own_rows, :]
            full[n * own_rows : (n + 1) * own_rows, pl.ds(start, columns)] = got
    first[...] = full[:own_rows, :]
    half = width // 2
    for n in range(in_chunk):
        at = slice(n * own_rows, (n + 1) * own_rows)
        widened = full[at, :].astype(jnp.float32)
        mean = jnp.sum(widened * widened, axis=-1, keepdims=True) / width
        normed = (widened * lax.rsqrt(mean + norm_eps) * gain[...]).astype(jnp.bfloat16)
        left[at, :] = normed[:, :half]
        right[at, :] = normed[:, half:]


def local(
    queries,
    new_latent,
    pool,
    page_list,
    prefix_len,
    hidden_in,
    norm_gain,
    uv_weight,
    out_weight,
    route_ids,
    route_weight,
    gate_weight,
    up_weight,
    down_weight,
):
    req_count = lax.axis_size("req")
    exp_count = lax.axis_size("exp")
    req_index = lax.axis_index("req")
    exp_index = lax.axis_index("exp")
    tok_rows = queries.shape[0]
    latent = new_latent.shape[1]
    kv_rank = uv_weight.shape[1]
    value_width = uv_weight.shape[2]
    head_here = uv_weight.shape[0]
    pool_rows = pool.shape[0]
    page_size = pool.shape[1] // latent
    list_depth = page_list.shape[1]
    per_index = page_list.shape[0] // req_count
    depth_here = list_depth // req_count
    width = hidden_in.shape[1]
    col_width = width // req_count
    half_width = width // 2
    own_rows = tok_rows // exp_count
    outer = exp_count // 2
    req_rel = req_index ^ jnp.arange(req_count, dtype=jnp.int32)
    rel_order = [2 * k for k in range(outer)] + [2 * k + 1 for k in range(outer)]
    exp_rel = exp_index ^ jnp.array(rel_order, dtype=jnp.int32)

    slots = per_index * depth_here
    pair = 2 * latent
    pool_width = pool.shape[1]
    far_width = pool_width // exp_count
    far_split = min(16 // slots, far_width // pair)
    near_split = 16 // slots
    lengths = prefix_len.reshape(req_count, per_index)
    place = jnp.stack([req_index, exp_index]).astype(jnp.int32)
    plan = (
        req_count, per_index, depth_here, pool_rows, pool_width, far_width, far_split, near_split,
    )
    scalars = pl.BlockSpec(memory_space=pltpu.SMEM)
    whole = pl.BlockSpec(memory_space=pltpu.VMEM)
    far_shape = jax.ShapeDtypeStruct((16, far_width // far_split), jnp.bfloat16)
    sent = pl.pallas_call(
        functools.partial(pick_kernel, plan),
        out_shape=[far_shape] * (req_count - 1),
        grid_spec=pltpu.PrefetchScalarGridSpec(
            num_scalar_prefetch=2,
            grid=(1,),
            in_specs=[pl.BlockSpec((pool_rows, far_width), lambda n, place, lists: (0, place[1]))],
            out_specs=[whole] * (req_count - 1),
        ),
        name="pick_far",
    )(place, page_list, pool)
    near = pl.pallas_call(
        functools.partial(near_kernel, plan),
        out_shape=jax.ShapeDtypeStruct((16, pool_width // near_split), jnp.bfloat16),
        in_specs=[scalars, scalars, whole],
        out_specs=whole,
        name="pick_near",
    )(place, page_list, pool)
    far = jnp.concatenate([swap(sent[j - 1], "req", j) for j in range(1, req_count)], axis=0)
    far_out = jnp.stack([far] + [swap(far, "exp", 2 * k) for k in range(1, outer)])
    far_all = jnp.concatenate([far_out, swap(far_out, "exp", 1)], axis=0)

    def positions(tokens, holder_ids, split, slot_row):
        depth = holder_ids * depth_here + slot_row % slots % depth_here
        return jnp.where(slot_row < slots * split, depth * page_size + tokens, list_depth * page_size)

    chosen = route_ids == exp_index
    token_weight = jnp.sum(jnp.where(chosen, route_weight, 0.0), axis=1)
    token_weight = token_weight.reshape(exp_count, own_rows)[exp_rel].reshape(-1)
    parts, left = [], token_weight
    for n in range(3):
        part = lax.reduce_precision(left, 8, 7)
        left = left - part
        parts.append(part.astype(jnp.bfloat16))
    head_cols = head_here * value_width
    extra_rows = -(-3 * tok_rows // (16 * head_cols)) * 16
    extra = jnp.concatenate(parts)
    extra = jnp.pad(extra, (0, extra_rows * head_cols - 3 * tok_rows))
    extra = extra.reshape(extra_rows, head_cols)

    near_piece = page_size // near_split
    pairs = np.arange(near_piece // 2)[:, None]
    slot_row = np.arange(16)[None, :]
    near_pos = positions(slot_row // slots * near_piece + 2 * pairs, req_index, near_split, slot_row)
    near_req = np.broadcast_to(slot_row % slots // depth_here, near_pos.shape)
    far_tokens = page_size // exp_count
    far_piece = far_tokens // far_split
    pairs = np.arange(far_piece // 2).reshape(1, -1, 1, 1)
    slot_row = np.arange(16).reshape(1, 1, 1, -1)
    far_pos = positions(
        exp_rel.reshape(-1, 1, 1, 1) * far_tokens + slot_row // slots * far_piece + 2 * pairs,
        req_rel[1:].reshape(1, 1, -1, 1),
        far_split,
        slot_row,
    )
    far_req = np.broadcast_to(slot_row % slots // depth_here, far_pos.shape)
    key_pos = jnp.concatenate([near_pos.reshape(1, -1), far_pos.reshape(1, -1)], axis=1)
    key_req = np.concatenate([near_req.reshape(1, -1), far_req.reshape(1, -1)], axis=1)
    my_lengths = lax.dynamic_index_in_dim(lengths, req_index, 0, keepdims=False)[:, None]
    same = key_req == np.arange(per_index)[:, None]
    bias_even = jnp.where(same & (key_pos < my_lengths), 0.0, -1e30)
    bias_odd = jnp.where(same & (key_pos + 1 < my_lengths), 0.0, -1e30)
    new_count = tok_rows // per_index
    tok = np.arange(tok_rows)
    seen = (tok[:, None] // new_count == tok // new_count) & (tok <= tok[:, None])
    bias_new = jnp.asarray(np.where(seen, 0.0, -1e30), jnp.float32)
    by_head = queries.reshape(tok_rows, head_here, latent).transpose(1, 0, 2)
    by_head = by_head.reshape(head_here * tok_rows, latent)
    q_even = jnp.pad(by_head, ((0, 0), (0, 64)))
    q_odd = jnp.pad(by_head, ((0, 0), (64, 0)))
    new_keys = jnp.pad(new_latent, ((0, 0), (0, 64)))
    key_count = key_req.shape[1]
    q_rows = head_here * tok_rows
    head_out = pl.pallas_call(
        functools.partial(
            attention_kernel,
            (
                per_index, latent, kv_rank, head_here, tok_rows, tuple(rel_order), own_rows,
            ),
        ),
        out_shape=jax.ShapeDtypeStruct((tok_rows + extra_rows, head_cols), jnp.bfloat16),
        in_specs=[scalars] + [whole] * 10,
        out_specs=whole,
        scratch_shapes=[
            pltpu.VMEM((key_count, latent + 64), jnp.bfloat16),
            pltpu.VMEM((key_count, latent + 64), jnp.bfloat16),
            pltpu.VMEM((q_rows, key_count), jnp.float32),
            pltpu.VMEM((q_rows, key_count), jnp.float32),
            pltpu.VMEM((tok_rows, head_cols), jnp.float32),
        ],
        compiler_params=pltpu.CompilerParams(vmem_limit_bytes=12 * 1024 * 1024),
        name="attention",
    )(place, near, far_all, new_keys, q_even, q_odd, bias_even, bias_odd, bias_new, uv_weight, extra)
    if own_rows % 8:
        ordered = head_out[:tok_rows].reshape(exp_count, own_rows, head_cols)[exp_rel]
        head_out = jnp.concatenate([ordered.reshape(tok_rows, head_cols), head_out[tok_rows:]])

    heads = [head_out] + [swap(head_out, "req", j) for j in range(1, req_count)]
    weight_all = jnp.stack([h[tok_rows:].reshape(-1)[: 3 * tok_rows] for h in heads])
    weight_all = weight_all.astype(jnp.float32).reshape(req_count, 3, exp_count, own_rows)
    weight_all = (weight_all[:, 0] + weight_all[:, 1] + weight_all[:, 2]).transpose(1, 0, 2)
    block = req_count * own_rows
    aligned = own_rows % 16 == 0 and outer == 4
    somewhere = pl.BlockSpec(memory_space=pl.ANY)
    in_hbm = pl.BlockSpec(memory_space=pltpu.HBM)
    cut = outer * block

    def grant(mib):
        return pltpu.CompilerParams(vmem_limit_bytes=mib * 1024 * 1024)

    def pair_blocks(keep, got):
        rows, columns = keep.shape[0] // 4, keep.shape[1]
        return pl.pallas_call(
            pair_kernel,
            out_shape=[jax.ShapeDtypeStruct((rows, columns), jnp.float32)]
            + [jax.ShapeDtypeStruct((rows, columns), jnp.bfloat16)] * 3
            + [jax.ShapeDtypeStruct((own_rows, columns), jnp.bfloat16)] * req_count,
            in_specs=[scalars, whole, whole, whole],
            out_specs=[whole] * (4 + req_count),
            compiler_params=grant(4),
            name="pair",
        )(place, keep, got, hidden_in)

    if aligned:
        keep, give = pl.pallas_call(
            functools.partial(project_kernel, (req_count, exp_count, own_rows)),
            out_shape=[
                jax.ShapeDtypeStruct((cut, col_width), jnp.float32),
                jax.ShapeDtypeStruct((cut, col_width), jnp.bfloat16),
            ],
            in_specs=[whole] * req_count + [in_hbm],
            out_specs=[whole, whole],
            scratch_shapes=[
                pltpu.VMEM((2 * cut, head_cols), jnp.bfloat16),
                pltpu.VMEM(out_weight.shape, jnp.bfloat16),
                pltpu.SemaphoreType.DMA,
            ],
            compiler_params=grant(6),
            name="project",
        )(*heads, out_weight)
        parts = pair_blocks(keep, swap(give, "exp", 1))
        parts, hidden = parts[:4], parts[4:]
    else:
        heads_all = jnp.stack(
            [h[:tok_rows].reshape(exp_count, own_rows, head_cols) for h in heads], axis=1
        )
        partial = jnp.dot(
            heads_all.reshape(exp_count * block, head_cols),
            out_weight,
            preferred_element_type=jnp.float32,
        )
        other = swap(partial[cut:].astype(jnp.bfloat16), "exp", 1)
        parts = partial[:cut] + other.astype(jnp.float32)
        parts = list(parts.reshape(outer, block, col_width))
    chunks = 2
    in_chunk = req_count // chunks
    chunk_block = in_chunk * own_rows
    along = [swap(parts[k].astype(jnp.bfloat16), "exp", 2 * k) for k in range(1, outer)]

    def collect(blocks, others):
        rows = sum(x.shape[0] for x in blocks)
        return pl.pallas_call(
            functools.partial(collect_kernel, len(blocks)),
            out_shape=jax.ShapeDtypeStruct((rows, blocks[0].shape[1]), blocks[0].dtype),
            in_specs=[whole] * len(blocks) + [somewhere] * len(others),
            out_specs=whole,
            compiler_params=grant(2),
            name="collect",
        )(*blocks, *others)

    def pick_blocks(blocks, picks, others):
        rows = sum(blocks[k].shape[-2] for k, n in picks)
        return pl.pallas_call(
            functools.partial(pick_blocks_kernel, picks, len(blocks)),
            out_shape=jax.ShapeDtypeStruct((rows, blocks[0].shape[-1]), blocks[0].dtype),
            in_specs=[whole] * len(blocks) + [somewhere] * len(others),
            out_specs=whole,
            compiler_params=grant(2),
            name="pick_blocks",
        )(*blocks, *others)

    if aligned and in_chunk == 2:
        hidden = [x if j == 0 else swap(x, "req", j) for j, x in enumerate(hidden)]
        resid = pl.pallas_call(
            resid_kernel,
            out_shape=[jax.ShapeDtypeStruct((chunk_block, col_width), jnp.bfloat16)] * chunks,
            in_specs=[whole] * (4 + req_count),
            out_specs=[whole] * chunks,
            compiler_params=grant(2),
            name="resid",
        )(parts[0], *along, *hidden)
        gain = norm_gain.astype(jnp.float32).reshape(1, width)

        def normalise(c, after_slices, after_norm):
            sent = resid
            if after_slices:
                sent = [collect([x], after_slices) for x in resid]
            slices = [resid[c]]
            for b in range(1, req_count):
                slices.append(swap(sent[c ^ b // in_chunk], "req", b))
            half_shape = jax.ShapeDtypeStruct((chunk_block, half_width), jnp.bfloat16)
            *halves, first = pl.pallas_call(
                functools.partial(norm_kernel, (req_count, own_rows, len(after_norm))),
                out_shape=[half_shape, half_shape]
                + [jax.ShapeDtypeStruct((own_rows, width), jnp.bfloat16)],
                in_specs=[scalars] + [whole] * (1 + req_count) + [somewhere] * len(after_norm),
                out_specs=[whole] * 3,
                scratch_shapes=[pltpu.VMEM((chunk_block, width), jnp.bfloat16)],
                compiler_params=grant(4),
                name="norm",
            )(place, gain, *slices, *after_norm)
            return slices, halves, first
    else:
        hidden = [
            lax.dynamic_slice_in_dim(hidden_in, req_rel[j] * col_width, col_width, 1)
            for j in range(req_count)
        ]
        hidden = [x if j == 0 else swap(x, "req", j) for j, x in enumerate(hidden)]
        attn = sum([x.astype(jnp.float32) for x in along], parts[0])
        resid = jnp.concatenate(hidden, axis=0).astype(jnp.float32) + attn
        resid = resid.astype(jnp.bfloat16)
        pieces = [resid]
        for b in range(1, req_count):
            got = swap(resid, "req", b).reshape(req_count, own_rows, col_width)
            pieces.append(jnp.concatenate([got[i ^ b] for i in range(req_count)], axis=0))
        full = jnp.stack(pieces)[req_rel].transpose(1, 0, 2).reshape(block, width)
        widened = full.astype(jnp.float32)
        inv_scale = lax.rsqrt(jnp.mean(widened * widened, axis=-1, keepdims=True) + norm_eps)
        normed = (widened * inv_scale * norm_gain.astype(jnp.float32)).astype(jnp.bfloat16)
        normed = normed.reshape(chunks, chunk_block, 2, half_width)

        def normalise(c, after_slices, after_norm):
            return [], [normed[c, :, n] for n in range(2)], full[:own_rows]

    outer_bits = []
    bit = 1
    while bit < outer:
        outer_bits.append(bit)
        bit *= 2
    orders = (outer_bits, outer_bits[::-1])

    def gather_plane(piece, bits):
        held, ids, trips = piece[None], [0], []
        for n, bit in enumerate(bits):
            if n:
                held = jnp.concatenate([held, trips[-1]], axis=0)
            trips.append(swap(held, "exp", 2 * bit))
            ids = ids + [k ^ bit for k in ids]
        return held, trips[-1], ids, trips[0]

    def finish_plane(held, got, ids, others, direct):
        if direct:
            picks = [divmod(ids.index(k), outer // 2) for k in range(outer)]
            same = pick_blocks([held, got], picks, others)
        else:
            held = jnp.concatenate([held, got], axis=0)
            same = [held[ids.index(k)] for k in range(outer)]
            same = collect(same, others) if others else jnp.concatenate(same, axis=0)
        return jnp.concatenate([same, swap(same, "exp", 1)], axis=0)

    def scatter_plane(partial, bits):
        cut = outer * chunk_block
        other = swap(partial[cut:].astype(jnp.bfloat16), "exp", 1)
        held = (partial[:cut] + other.astype(jnp.float32)).reshape(outer, chunk_block, half_width)
        ids = list(range(outer))
        firsts = []
        for bit in bits:
            keep = [n for n, k in enumerate(ids) if not k & bit]
            give = [ids.index(ids[n] ^ bit) for n in keep]
            sent = swap(jnp.stack([held[n] for n in give]).astype(jnp.bfloat16), "exp", 2 * bit)
            firsts.append(sent)
            held = jnp.stack([held[n] for n in keep]) + sent.astype(jnp.float32)
            ids = [ids[n] for n in keep]
        return held[0].astype(jnp.bfloat16), firsts[0]

    gate_here = gate_weight[0]
    up_here = up_weight[0]
    down_here = down_weight[0]
    total = 0.0
    slices, halves, resid_own = normalise(1, [], [])
    parts = [gather_plane(halves[n], orders[n]) for n in range(2)]
    early = [finish_plane(*part[:3], [], False) for part in parts]
    slices, halves, resid_own = normalise(0, slices[1:], [part[3] for part in parts])
    late_parts = [gather_plane(halves[n], orders[n]) for n in range(2)]

    def products(rows, c, before_down):
        left, right = rows

        def project(matrix):
            return jnp.dot(
                left, matrix[:half_width], preferred_element_type=jnp.float32
            ) + jnp.dot(right, matrix[half_width:], preferred_element_type=jnp.float32)

        gate_val, up_val = project(gate_here), project(up_here)
        active = (jax.nn.silu(gate_val) * up_val).astype(jnp.bfloat16)
        if before_down:
            active = collect([active], before_down)
        reqs = range(c * in_chunk, (c + 1) * in_chunk)
        row_weight = weight_all[:, reqs[0] : reqs[-1] + 1].reshape(-1, 1)
        outs = []
        for n in range(2):
            cols = slice(n * half_width, (n + 1) * half_width)
            out = jnp.dot(active, down_here[:, cols], preferred_element_type=jnp.float32)
            outs.append(out * row_weight)
        return outs

    def spread(outs, c):
        nonlocal total
        sides, firsts = [], []
        for n in range(2):
            side, first = scatter_plane(outs[n], orders[n])
            sides.append(side)
            firsts.append(first)
        sums = jnp.concatenate(sides, axis=1)
        for n, j in reversed(list(enumerate(range(c * in_chunk, (c + 1) * in_chunk)))):
            part = sums[n * own_rows : (n + 1) * own_rows]
            if j:
                part = swap(part, "req", j)
            total = total + part.astype(jnp.float32)
        return firsts

    early_outs = products(early, 1, [])
    late = [
        finish_plane(*part[:3], early_outs, n == 0) for n, part in enumerate(late_parts)
    ]
    firsts = spread(early_outs, 1)
    late_outs = products(late, 0, firsts)
    spread(late_outs, 0)
    return (total + resid_own.astype(jnp.float32)).astype(jnp.bfloat16)


def solution(mesh):
    return jax.shard_map(
        local,
        mesh=mesh,
        in_specs=(
            P("req", "exp"),
            P("req", None),
            P("req", None),
            P(),
            P(),
            P(("req", "exp"), None),
            P(),
            P("exp", None, None),
            P("exp", "req"),
            P("req", None),
            P("req", None),
            P("exp", None, "req"),
            P("exp", None, "req"),
            P("exp", "req", None),
        ),
        out_specs=P(("req", "exp"), None),
        check_vma=False,
    )
```

```python
import functools

import jax
import jax.numpy as jnp
import numpy as np
from jax import lax
from jax.experimental import pallas as pl
from jax.experimental.pallas import tpu as pltpu
from jax.sharding import PartitionSpec as P

score_scale = 192.0 ** (-0.5)
norm_eps = 1e-06


def swap(x, axis, distance):
    size = lax.axis_size(axis)
    return lax.ppermute(x, axis, [(i, i ^ distance) for i in range(size)])


def pick_kernel(plan, place, lists, pool, *outs):
    req_count, per_index, depth_here, pool_rows, width, far_width, far_split, near_split = plan
    slots = per_index * depth_here
    req_index = place[0]
    row = lax.broadcasted_iota(jnp.int32, (16, pool_rows), 0)
    column = lax.broadcasted_iota(jnp.int32, (16, pool_rows), 1)

    def wanted(target):
        hot = row < 0
        for slot in range(slots):
            request, depth = slot // depth_here, slot % depth_here
            page = lists[target * per_index + request, req_index * depth_here + depth]
            hot = hot | ((row == slot) & (column == page - req_index * pool_rows))
        return hot.astype(jnp.float32)

    piece = far_width // far_split
    for out, j in zip(outs, range(1, req_count)):
        hot = wanted(req_index ^ j)
        total = jnp.zeros((16, piece), jnp.float32)
        for part in range(far_split):
            shifted = hot if part == 0 else pltpu.roll(hot, part * slots, 0)
            total = total + jnp.dot(
                shifted.astype(jnp.bfloat16),
                pool[:, part * piece : (part + 1) * piece],
                preferred_element_type=jnp.float32,
            )
        out[...] = total.astype(jnp.bfloat16)


def near_kernel(plan, place, lists, pool, out):
    req_count, per_index, depth_here, pool_rows, width, far_width, far_split, near_split = plan
    slots = per_index * depth_here
    req_index = place[0]
    row = lax.broadcasted_iota(jnp.int32, (16, pool_rows), 0)
    column = lax.broadcasted_iota(jnp.int32, (16, pool_rows), 1)
    hots = [row < 0] * near_split
    for slot in range(slots):
        request, depth = slot // depth_here, slot % depth_here
        page = lists[req_index * per_index + request, req_index * depth_here + depth]
        here = column == page - req_index * pool_rows
        for part in range(near_split):
            hots[part] = hots[part] | ((row == part * slots + slot) & here)
    hots = [hot.astype(jnp.float32).astype(jnp.bfloat16) for hot in hots]
    piece = width // near_split
    step = 1152
    for start in range(0, piece, step):
        total = jnp.zeros((16, step), jnp.float32)
        for part in range(near_split):
            cols = slice(part * piece + start, part * piece + start + step)
            total = total + jnp.dot(hots[part], pool[:, cols], preferred_element_type=jnp.float32)
        out[:, start : start + step] = total.astype(jnp.bfloat16)


def attention_kernel(
    plan, place, near, far, new, q_even, q_odd, bias_even, bias_odd, bias_new, uv, extra, out,
    k_even, k_odd, s_even, s_odd, heads,
):
    per_index, latent, kv_rank, head_here, tok_rows, order, own_rows = plan
    pair = 2 * latent
    window = latent + 64
    lead = pair - window
    units, far_rows, far_width = far.shape
    near_rows = near.shape[0]
    base = 0

    def place_keys(rows, value_of, pairs, base):
        for p in range(pairs):
            k_even[base : base + rows, :] = value_of(p * pair, p * pair + window)
            k_odd[base : base + rows, :] = value_of(p * pair + lead, (p + 1) * pair)
            base += rows
        return base

    base = place_keys(near_rows, lambda a, b: near[:, a:b], near.shape[1] // pair, base)
    for m in range(units):
        base = place_keys(far_rows, lambda a, b: far[m, :, a:b], far_width // pair, base)
    rows_k = (((1,), (1,)), ((), ()))

    def times(a, b):
        return lax.dot_general(a, b, rows_k, preferred_element_type=jnp.float32) * score_scale

    s_even[...] = times(q_even[...], k_even[...])
    s_odd[...] = times(q_odd[...], k_odd[...])
    s_new = times(q_even[...], new[...])
    new_count = tok_rows // per_index
    p_even, p_odd, p_new = [], [], []
    for h in range(head_here):
        for i in range(per_index):
            at = h * tok_rows + i * new_count
            rows = slice(at, at + new_count)
            even = s_even[rows, :] + bias_even[i : i + 1, :]
            odd = s_odd[rows, :] + bias_odd[i : i + 1, :]
            fresh = s_new[rows, :] + bias_new[i * new_count : (i + 1) * new_count, :]
            top = jnp.maximum(
                jnp.max(jnp.maximum(even, odd), axis=-1, keepdims=True),
                jnp.max(fresh, axis=-1, keepdims=True),
            )
            even, odd, fresh = jnp.exp(even - top), jnp.exp(odd - top), jnp.exp(fresh - top)
            share = 1.0 / (
                jnp.sum(even + odd, axis=-1, keepdims=True)
                + jnp.sum(fresh, axis=-1, keepdims=True)
            )
            p_even.append((even * share).astype(jnp.bfloat16))
            p_odd.append((odd * share).astype(jnp.bfloat16))
            p_new.append((fresh * share).astype(jnp.bfloat16))
    p_even, p_odd, p_new = (jnp.concatenate(p, axis=0) for p in (p_even, p_odd, p_new))
    first = jnp.dot(p_even, k_even[:, :kv_rank], preferred_element_type=jnp.float32)
    second = jnp.dot(p_odd, k_odd[...], preferred_element_type=jnp.float32)
    third = jnp.dot(p_new, new[:, :kv_rank], preferred_element_type=jnp.float32)
    latent_out = (first + third + second[:, 64 : 64 + kv_rank]).astype(jnp.bfloat16)
    value_width = uv.shape[2]
    for h in range(head_here):
        heads[:, h * value_width : (h + 1) * value_width] = jnp.dot(
            latent_out[h * tok_rows : (h + 1) * tok_rows],
            uv[h],
            preferred_element_type=jnp.float32,
        )
    out[tok_rows:, :] = extra[...]
    if own_rows % 8:
        out[:tok_rows, :] = heads[...].astype(jnp.bfloat16)
        return
    exp_index = place[1]
    blocks = []
    for m in order:
        at = (exp_index ^ m) * own_rows
        blocks.append(heads[pl.ds(pl.multiple_of(at, 8), own_rows), :])
    out[:tok_rows, :] = jnp.concatenate(blocks, axis=0).astype(jnp.bfloat16)


def hold_kernel(x, other, out):
    del other
    out[...] = x[...]


def collect_kernel(count, *refs):
    out, base = refs[-1], 0
    for ref in refs[:count]:
        out[base : base + ref.shape[0], :] = ref[...]
        base += ref.shape[0]


def pick_blocks_kernel(picks, count, *refs):
    out, base = refs[-1], 0
    for k, n in picks:
        rows = refs[k].shape[-2]
        out[base : base + rows, :] = refs[k][n]
        base += rows


def project_kernel(plan, *refs):
    req_count, exp_count, own_rows = plan
    heads, (weight, keep, give, rows, held, sem) = refs[:req_count], refs[req_count:]
    fetch = pltpu.make_async_copy(weight, held, sem)
    fetch.start()
    for j in range(req_count):
        for m in range(exp_count):
            at = (m * req_count + j) * own_rows
            rows[at : at + own_rows, :] = heads[j][m * own_rows : (m + 1) * own_rows, :]
    fetch.wait()
    half = keep.shape[0]
    for n in range(0, keep.shape[1], 256):
        cols = slice(n, n + 256)
        out = jnp.dot(rows[...], held[:, cols], preferred_element_type=jnp.float32)
        keep[:, cols] = out[:half]
        give[:, cols] = out[half:].astype(jnp.bfloat16)


def pair_kernel(place, keep, got, hidden, *outs):
    rows = outs[0].shape[0]
    for k, out in enumerate(outs[:4]):
        at = slice(k * rows, (k + 1) * rows)
        out[...] = (keep[at, :] + got[at, :].astype(jnp.float32)).astype(out.dtype)
    columns = outs[0].shape[1]
    for j, out in enumerate(outs[4:]):
        start = pl.multiple_of((place[0] ^ j) * columns, 128)
        out[...] = hidden[:, pl.ds(start, columns)]


def resid_kernel(own, *refs):
    req_count = 4
    sums, hidden, outs = refs[:3], refs[3 : 3 + req_count], refs[3 + req_count :]
    rows = hidden[0].shape[0]
    in_chunk = req_count // len(outs)
    for j in range(req_count):
        at = slice(j * rows, (j + 1) * rows)
        total = own[at, :]
        for ref in sums:
            total = total + ref[at, :].astype(jnp.float32)
        total = (hidden[j][...].astype(jnp.float32) + total).astype(jnp.bfloat16)
        to = j % in_chunk * rows
        outs[j // in_chunk][to : to + rows, :] = total


def norm_kernel(plan, place, gain, *refs):
    req_count, own_rows, others = plan
    pieces, (left, right, first, full) = refs[:req_count], refs[req_count + others :]
    rows, columns = pieces[0].shape
    in_chunk = rows // own_rows
    width = columns * req_count
    for b, piece in enumerate(pieces):
        start = pl.multiple_of((place[0] ^ b) * columns, 128)
        for n in range(in_chunk):
            m = n ^ (b % in_chunk)
            got = piece[m * own_rows : (m + 1) * own_rows, :]
            full[n * own_rows : (n + 1) * own_rows, pl.ds(start, columns)] = got
    first[...] = full[:own_rows, :]
    half = width // 2
    for n in range(in_chunk):
        at = slice(n * own_rows, (n + 1) * own_rows)
        widened = full[at, :].astype(jnp.float32)
        mean = jnp.sum(widened * widened, axis=-1, keepdims=True) / width
        normed = (widened * lax.rsqrt(mean + norm_eps) * gain[...]).astype(jnp.bfloat16)
        left[at, :] = normed[:, :half]
        right[at, :] = normed[:, half:]


def local(
    queries,
    new_latent,
    pool,
    page_list,
    prefix_len,
    hidden_in,
    norm_gain,
    uv_weight,
    out_weight,
    route_ids,
    route_weight,
    gate_weight,
    up_weight,
    down_weight,
):
    req_count = lax.axis_size("req")
    exp_count = lax.axis_size("exp")
    req_index = lax.axis_index("req")
    exp_index = lax.axis_index("exp")
    tok_rows = queries.shape[0]
    latent = new_latent.shape[1]
    kv_rank = uv_weight.shape[1]
    value_width = uv_weight.shape[2]
    head_here = uv_weight.shape[0]
    pool_rows = pool.shape[0]
    page_size = pool.shape[1] // latent
    list_depth = page_list.shape[1]
    per_index = page_list.shape[0] // req_count
    depth_here = list_depth // req_count
    width = hidden_in.shape[1]
    col_width = width // req_count
    half_width = width // 2
    own_rows = tok_rows // exp_count
    outer = exp_count // 2
    req_rel = req_index ^ jnp.arange(req_count, dtype=jnp.int32)
    rel_order = [2 * k for k in range(outer)] + [2 * k + 1 for k in range(outer)]
    exp_rel = exp_index ^ jnp.array(rel_order, dtype=jnp.int32)

    slots = per_index * depth_here
    pair = 2 * latent
    pool_width = pool.shape[1]
    far_width = pool_width // exp_count
    far_split = min(16 // slots, far_width // pair)
    near_split = 16 // slots
    lengths = prefix_len.reshape(req_count, per_index)
    place = jnp.stack([req_index, exp_index]).astype(jnp.int32)
    plan = (
        req_count, per_index, depth_here, pool_rows, pool_width, far_width, far_split, near_split,
    )
    scalars = pl.BlockSpec(memory_space=pltpu.SMEM)
    whole = pl.BlockSpec(memory_space=pltpu.VMEM)
    far_shape = jax.ShapeDtypeStruct((16, far_width // far_split), jnp.bfloat16)
    sent = pl.pallas_call(
        functools.partial(pick_kernel, plan),
        out_shape=[far_shape] * (req_count - 1),
        grid_spec=pltpu.PrefetchScalarGridSpec(
            num_scalar_prefetch=2,
            grid=(1,),
            in_specs=[pl.BlockSpec((pool_rows, far_width), lambda n, place, lists: (0, place[1]))],
            out_specs=[whole] * (req_count - 1),
        ),
        name="pick_far",
    )(place, page_list, pool)
    near = pl.pallas_call(
        functools.partial(near_kernel, plan),
        out_shape=jax.ShapeDtypeStruct((16, pool_width // near_split), jnp.bfloat16),
        in_specs=[scalars, scalars, whole],
        out_specs=whole,
        name="pick_near",
    )(place, page_list, pool)
    far = jnp.concatenate([swap(sent[j - 1], "req", j) for j in range(1, req_count)], axis=0)
    far_out = jnp.stack([far] + [swap(far, "exp", 2 * k) for k in range(1, outer)])
    far_all = jnp.concatenate([far_out, swap(far_out, "exp", 1)], axis=0)

    def positions(tokens, holder_ids, split, slot_row):
        depth = holder_ids * depth_here + slot_row % slots % depth_here
        return jnp.where(slot_row < slots * split, depth * page_size + tokens, list_depth * page_size)

    chosen = route_ids == exp_index
    token_weight = jnp.sum(jnp.where(chosen, route_weight, 0.0), axis=1)
    token_weight = token_weight.reshape(exp_count, own_rows)[exp_rel].reshape(-1)
    parts, left = [], token_weight
    for n in range(3):
        part = lax.reduce_precision(left, 8, 7)
        left = left - part
        parts.append(part.astype(jnp.bfloat16))
    head_cols = head_here * value_width
    extra_rows = -(-3 * tok_rows // (16 * head_cols)) * 16
    extra = jnp.concatenate(parts)
    extra = jnp.pad(extra, (0, extra_rows * head_cols - 3 * tok_rows))
    extra = extra.reshape(extra_rows, head_cols)

    near_piece = page_size // near_split
    pairs = np.arange(near_piece // 2)[:, None]
    slot_row = np.arange(16)[None, :]
    near_pos = positions(slot_row // slots * near_piece + 2 * pairs, req_index, near_split, slot_row)
    near_req = np.broadcast_to(slot_row % slots // depth_here, near_pos.shape)
    far_tokens = page_size // exp_count
    far_piece = far_tokens // far_split
    pairs = np.arange(far_piece // 2).reshape(1, -1, 1, 1)
    slot_row = np.arange(16).reshape(1, 1, 1, -1)
    far_pos = positions(
        exp_rel.reshape(-1, 1, 1, 1) * far_tokens + slot_row // slots * far_piece + 2 * pairs,
        req_rel[1:].reshape(1, 1, -1, 1),
        far_split,
        slot_row,
    )
    far_req = np.broadcast_to(slot_row % slots // depth_here, far_pos.shape)
    key_pos = jnp.concatenate([near_pos.reshape(1, -1), far_pos.reshape(1, -1)], axis=1)
    key_req = np.concatenate([near_req.reshape(1, -1), far_req.reshape(1, -1)], axis=1)
    my_lengths = lax.dynamic_index_in_dim(lengths, req_index, 0, keepdims=False)[:, None]
    same = key_req == np.arange(per_index)[:, None]
    bias_even = jnp.where(same & (key_pos < my_lengths), 0.0, -1e30)
    bias_odd = jnp.where(same & (key_pos + 1 < my_lengths), 0.0, -1e30)
    new_count = tok_rows // per_index
    tok = np.arange(tok_rows)
    seen = (tok[:, None] // new_count == tok // new_count) & (tok <= tok[:, None])
    bias_new = jnp.asarray(np.where(seen, 0.0, -1e30), jnp.float32)
    by_head = queries.reshape(tok_rows, head_here, latent).transpose(1, 0, 2)
    by_head = by_head.reshape(head_here * tok_rows, latent)
    q_even = jnp.pad(by_head, ((0, 0), (0, 64)))
    q_odd = jnp.pad(by_head, ((0, 0), (64, 0)))
    new_keys = jnp.pad(new_latent, ((0, 0), (0, 64)))
    key_count = key_req.shape[1]
    q_rows = head_here * tok_rows
    head_out = pl.pallas_call(
        functools.partial(
            attention_kernel,
            (
                per_index, latent, kv_rank, head_here, tok_rows, tuple(rel_order), own_rows,
            ),
        ),
        out_shape=jax.ShapeDtypeStruct((tok_rows + extra_rows, head_cols), jnp.bfloat16),
        in_specs=[scalars] + [whole] * 10,
        out_specs=whole,
        scratch_shapes=[
            pltpu.VMEM((key_count, latent + 64), jnp.bfloat16),
            pltpu.VMEM((key_count, latent + 64), jnp.bfloat16),
            pltpu.VMEM((q_rows, key_count), jnp.float32),
            pltpu.VMEM((q_rows, key_count), jnp.float32),
            pltpu.VMEM((tok_rows, head_cols), jnp.float32),
        ],
        compiler_params=pltpu.CompilerParams(vmem_limit_bytes=12 * 1024 * 1024),
        name="attention",
    )(place, near, far_all, new_keys, q_even, q_odd, bias_even, bias_odd, bias_new, uv_weight, extra)
    if own_rows % 8:
        ordered = head_out[:tok_rows].reshape(exp_count, own_rows, head_cols)[exp_rel]
        head_out = jnp.concatenate([ordered.reshape(tok_rows, head_cols), head_out[tok_rows:]])

    heads = [head_out] + [swap(head_out, "req", j) for j in range(1, req_count)]
    weight_all = jnp.stack([h[tok_rows:].reshape(-1)[: 3 * tok_rows] for h in heads])
    weight_all = weight_all.astype(jnp.float32).reshape(req_count, 3, exp_count, own_rows)
    weight_all = (weight_all[:, 0] + weight_all[:, 1] + weight_all[:, 2]).transpose(1, 0, 2)
    block = req_count * own_rows
    aligned = own_rows % 16 == 0 and outer == 4
    somewhere = pl.BlockSpec(memory_space=pl.ANY)
    in_hbm = pl.BlockSpec(memory_space=pltpu.HBM)
    cut = outer * block

    def grant(mib):
        return pltpu.CompilerParams(vmem_limit_bytes=mib * 1024 * 1024)

    def pair_blocks(keep, got):
        rows, columns = keep.shape[0] // 4, keep.shape[1]
        return pl.pallas_call(
            pair_kernel,
            out_shape=[jax.ShapeDtypeStruct((rows, columns), jnp.float32)]
            + [jax.ShapeDtypeStruct((rows, columns), jnp.bfloat16)] * 3
            + [jax.ShapeDtypeStruct((own_rows, columns), jnp.bfloat16)] * req_count,
            in_specs=[scalars, whole, whole, whole],
            out_specs=[whole] * (4 + req_count),
            compiler_params=grant(4),
            name="pair",
        )(place, keep, got, hidden_in)

    if aligned:
        keep, give = pl.pallas_call(
            functools.partial(project_kernel, (req_count, exp_count, own_rows)),
            out_shape=[
                jax.ShapeDtypeStruct((cut, col_width), jnp.float32),
                jax.ShapeDtypeStruct((cut, col_width), jnp.bfloat16),
            ],
            in_specs=[whole] * req_count + [in_hbm],
            out_specs=[whole, whole],
            scratch_shapes=[
                pltpu.VMEM((2 * cut, head_cols), jnp.bfloat16),
                pltpu.VMEM(out_weight.shape, jnp.bfloat16),
                pltpu.SemaphoreType.DMA,
            ],
            compiler_params=grant(6),
            name="project",
        )(*heads, out_weight)
        parts = pair_blocks(keep, swap(give, "exp", 1))
        parts, hidden = parts[:4], parts[4:]
    else:
        heads_all = jnp.stack(
            [h[:tok_rows].reshape(exp_count, own_rows, head_cols) for h in heads], axis=1
        )
        partial = jnp.dot(
            heads_all.reshape(exp_count * block, head_cols),
            out_weight,
            preferred_element_type=jnp.float32,
        )
        other = swap(partial[cut:].astype(jnp.bfloat16), "exp", 1)
        parts = partial[:cut] + other.astype(jnp.float32)
        parts = list(parts.reshape(outer, block, col_width))
    chunks = 2
    in_chunk = req_count // chunks
    chunk_block = in_chunk * own_rows
    along = [swap(parts[k].astype(jnp.bfloat16), "exp", 2 * k) for k in range(1, outer)]

    def collect(blocks, others):
        rows = sum(x.shape[0] for x in blocks)
        return pl.pallas_call(
            functools.partial(collect_kernel, len(blocks)),
            out_shape=jax.ShapeDtypeStruct((rows, blocks[0].shape[1]), blocks[0].dtype),
            in_specs=[whole] * len(blocks) + [somewhere] * len(others),
            out_specs=whole,
            compiler_params=grant(2),
            name="collect",
        )(*blocks, *others)

    def pick_blocks(blocks, picks, others):
        rows = sum(blocks[k].shape[-2] for k, n in picks)
        return pl.pallas_call(
            functools.partial(pick_blocks_kernel, picks, len(blocks)),
            out_shape=jax.ShapeDtypeStruct((rows, blocks[0].shape[-1]), blocks[0].dtype),
            in_specs=[whole] * len(blocks) + [somewhere] * len(others),
            out_specs=whole,
            compiler_params=grant(2),
            name="pick_blocks",
        )(*blocks, *others)

    if aligned and in_chunk == 2:
        hidden = [x if j == 0 else swap(x, "req", j) for j, x in enumerate(hidden)]
        resid = pl.pallas_call(
            resid_kernel,
            out_shape=[jax.ShapeDtypeStruct((chunk_block, col_width), jnp.bfloat16)] * chunks,
            in_specs=[whole] * (4 + req_count),
            out_specs=[whole] * chunks,
            compiler_params=grant(2),
            name="resid",
        )(parts[0], *along, *hidden)
        gain = norm_gain.astype(jnp.float32).reshape(1, width)

        def normalise(c, after_slices, after_norm):
            sent = resid
            if after_slices:
                sent = [collect([x], after_slices) for x in resid]
            slices = [resid[c]]
            for b in range(1, req_count):
                slices.append(swap(sent[c ^ b // in_chunk], "req", b))
            half_shape = jax.ShapeDtypeStruct((chunk_block, half_width), jnp.bfloat16)
            *halves, first = pl.pallas_call(
                functools.partial(norm_kernel, (req_count, own_rows, len(after_norm))),
                out_shape=[half_shape, half_shape]
                + [jax.ShapeDtypeStruct((own_rows, width), jnp.bfloat16)],
                in_specs=[scalars] + [whole] * (1 + req_count) + [somewhere] * len(after_norm),
                out_specs=[whole] * 3,
                scratch_shapes=[pltpu.VMEM((chunk_block, width), jnp.bfloat16)],
                compiler_params=grant(4),
                name="norm",
            )(place, gain, *slices, *after_norm)
            return slices, halves, first
    else:
        hidden = [
            lax.dynamic_slice_in_dim(hidden_in, req_rel[j] * col_width, col_width, 1)
            for j in range(req_count)
        ]
        hidden = [x if j == 0 else swap(x, "req", j) for j, x in enumerate(hidden)]
        attn = sum([x.astype(jnp.float32) for x in along], parts[0])
        resid = jnp.concatenate(hidden, axis=0).astype(jnp.float32) + attn
        resid = resid.astype(jnp.bfloat16)
        pieces = [resid]
        for b in range(1, req_count):
            got = swap(resid, "req", b).reshape(req_count, own_rows, col_width)
            pieces.append(jnp.concatenate([got[i ^ b] for i in range(req_count)], axis=0))
        full = jnp.stack(pieces)[req_rel].transpose(1, 0, 2).reshape(block, width)
        widened = full.astype(jnp.float32)
        inv_scale = lax.rsqrt(jnp.mean(widened * widened, axis=-1, keepdims=True) + norm_eps)
        normed = (widened * inv_scale * norm_gain.astype(jnp.float32)).astype(jnp.bfloat16)
        normed = normed.reshape(chunks, chunk_block, 2, half_width)

        def normalise(c, after_slices, after_norm):
            return [], [normed[c, :, n] for n in range(2)], full[:own_rows]

    outer_bits = []
    bit = 1
    while bit < outer:
        outer_bits.append(bit)
        bit *= 2
    orders = (outer_bits, outer_bits[::-1])

    def gather_plane(piece, bits):
        held, ids, trips = piece[None], [0], []
        for n, bit in enumerate(bits):
            if n:
                held = jnp.concatenate([held, trips[-1]], axis=0)
            trips.append(swap(held, "exp", 2 * bit))
            ids = ids + [k ^ bit for k in ids]
        return held, trips[-1], ids, trips[0]

    def finish_plane(held, got, ids, others, direct):
        if direct:
            picks = [divmod(ids.index(k), outer // 2) for k in range(outer)]
            same = pick_blocks([held, got], picks, others)
        else:
            held = jnp.concatenate([held, got], axis=0)
            same = [held[ids.index(k)] for k in range(outer)]
            same = collect(same, others) if others else jnp.concatenate(same, axis=0)
        return jnp.concatenate([same, swap(same, "exp", 1)], axis=0)

    def scatter_plane(partial, bits):
        cut = outer * chunk_block
        other = swap(partial[cut:].astype(jnp.bfloat16), "exp", 1)
        held = (partial[:cut] + other.astype(jnp.float32)).reshape(outer, chunk_block, half_width)
        ids = list(range(outer))
        firsts = []
        for bit in bits:
            keep = [n for n, k in enumerate(ids) if not k & bit]
            give = [ids.index(ids[n] ^ bit) for n in keep]
            sent = swap(jnp.stack([held[n] for n in give]).astype(jnp.bfloat16), "exp", 2 * bit)
            firsts.append(sent)
            held = jnp.stack([held[n] for n in keep]) + sent.astype(jnp.float32)
            ids = [ids[n] for n in keep]
        return held[0].astype(jnp.bfloat16), firsts[0]

    gate_here = gate_weight[0]
    up_here = up_weight[0]
    down_here = down_weight[0]
    total = 0.0
    slices, halves, resid_own = normalise(1, [], [])
    parts = [gather_plane(halves[n], orders[n]) for n in range(2)]
    early = [finish_plane(*part[:3], [], False) for part in parts]
    slices, halves, resid_own = normalise(0, slices[1:], [part[3] for part in parts])
    late_parts = [gather_plane(halves[n], orders[n]) for n in range(2)]

    def products(rows, c, before_down):
        left, right = rows

        def project(matrix):
            return jnp.dot(
                left, matrix[:half_width], preferred_element_type=jnp.float32
            ) + jnp.dot(right, matrix[half_width:], preferred_element_type=jnp.float32)

        gate_val, up_val = project(gate_here), project(up_here)
        active = (jax.nn.silu(gate_val) * up_val).astype(jnp.bfloat16)
        reqs = range(c * in_chunk, (c + 1) * in_chunk)
        row_weight = weight_all[:, reqs[0] : reqs[-1] + 1].reshape(-1, 1)
        outs = []
        for n in range(2):
            cols = slice(n * half_width, (n + 1) * half_width)
            out = jnp.dot(active, down_here[:, cols], preferred_element_type=jnp.float32)
            outs.append(out * row_weight)
        return outs

    def spread(outs, c):
        nonlocal total
        sides, firsts = [], []
        for n in range(2):
            side, first = scatter_plane(outs[n], orders[n])
            sides.append(side)
            firsts.append(first)
        sums = jnp.concatenate(sides, axis=1)
        for n, j in reversed(list(enumerate(range(c * in_chunk, (c + 1) * in_chunk)))):
            part = sums[n * own_rows : (n + 1) * own_rows]
            if j:
                part = swap(part, "req", j)
            total = total + part.astype(jnp.float32)
        return firsts

    early_outs = products(early, 1, [])
    late = [
        finish_plane(*part[:3], early_outs, n == 0) for n, part in enumerate(late_parts)
    ]
    firsts = spread(early_outs, 1)
    late_outs = products(late, 0, firsts)
    spread(late_outs, 0)
    return (total + resid_own.astype(jnp.float32)).astype(jnp.bfloat16)


def solution(mesh):
    return jax.shard_map(
        local,
        mesh=mesh,
        in_specs=(
            P("req", "exp"),
            P("req", None),
            P("req", None),
            P(),
            P(),
            P(("req", "exp"), None),
            P(),
            P("exp", None, None),
            P("exp", "req"),
            P("req", None),
            P("req", None),
            P("exp", None, "req"),
            P("exp", None, "req"),
            P("exp", "req", None),
        ),
        out_specs=P(("req", "exp"), None),
        check_vma=False,
    )
```
